256 devices in a mesh: row: 4 (over x), col: 2 (over core), layer: 32 (over z, y).
Axes of the slice: x: 4, y: 4, z: 8, core: 2. Of those that a mesh axis runs over, the one named last changes fastest.
Arguments:
- a_matrix: bfloat16 [8192, 8192], P('row', ('col', 'layer')), may hold values from 0 to 9
- b_matrix: bfloat16 [8192, 8192], P(('col', 'row'), 'layer'), may hold values from 0 to 3
- tile_map: int32 [64, 64], P('row', ('col', 'layer')), may hold values from 0 to 1, as said below
Outputs:
- inflated: float32 [8192, 8192], P(('row', 'col'), 'layer')
The draws below stay inside these ranges and needn't reach their ends.
Inputs may be any that keep to these rules, and one draw needn't show every extreme that they name: Each device's shard of tile_map (16 entries) holds between 1 and 8 present tiles, and some shard holds exactly 8.
All inputs are finite; a program needn't handle non-finite values.
Results may differ from the reference program's by a relative error of at most 0.0003.
Values may be sent and summed in bfloat16 or wider, within the bound.
No kernel may reach another device: no remote copies, remote signals or barrier semaphores. Data moves between devices by JAX's collectives and lax.ppermute only.
A program may use at most 64 MiB of HBM per device.

```python
import math
import jax
import jax.numpy as jnp

TILE = 128
TPD = 1
N = 8192
TILES_DEV = 16
CAP = 8
N_ROW = 4
N_COL = 2
N_LAYER = 32


def level_field(key, spread):
    tiles = N // TILE
    level = jnp.exp(jax.random.uniform(key, (tiles, tiles), jnp.float32, -spread, spread))
    return jnp.repeat(jnp.repeat(level, TILE, 0), TILE, 1)


def draw_a_matrix(key, part):
    key = jax.random.fold_in(key, 11)
    first, second = jax.random.split(key)
    entry = jnp.exp(jax.random.uniform(first, (N, N), jnp.float32, math.log(0.05), 0.0))
    slope = 2.0
    rise = jnp.sqrt(1.0 + slope * jnp.arange(N, dtype=jnp.float32) / (N - 1))
    return (rise[:, None] * level_field(second, 1.0) * entry).astype(jnp.bfloat16)


def draw_b_matrix(key, part):
    key = jax.random.fold_in(key, 29)
    first, second = jax.random.split(key)
    entry = jnp.exp(jax.random.uniform(first, (N, N), jnp.float32, math.log(0.05), 0.0))
    return (level_field(second, 1.0) * entry).astype(jnp.bfloat16)


def draw_tile_map(key, part):
    key = jax.random.fold_in(key, 41)
    first, second, third, fourth = jax.random.split(key, 4)
    blocks = N_ROW * N_COL * N_LAYER
    shard_rows = TILES_DEV // TPD
    upper = jax.random.randint(first, (blocks,), 0, CAP)
    lower = jax.random.randint(second, (blocks,), 0, CAP)
    counts = 1 + upper * lower // CAP
    forced = jax.random.randint(third, (), 0, blocks)
    counts = jnp.where(jnp.arange(blocks) == forced, CAP, counts)
    scores = jax.random.randint(fourth, (blocks, TILES_DEV), 0, 1 << 20) * TILES_DEV
    scores = scores + jnp.arange(TILES_DEV, dtype=jnp.int32)[None, :]
    ranks = jnp.argsort(jnp.argsort(scores, axis=1), axis=1)
    present = (ranks < counts[:, None]).astype(jnp.int32)
    present = present.reshape(N_ROW, N_COL * N_LAYER, shard_rows, TPD).transpose(0, 2, 1, 3)
    return present.reshape(N // TILE, N // TILE)


def setup_inputs(seed: int = 0) -> dict:
    streams_of = jax.random.split(jax.random.key(seed), 4)
    a_matrix = draw_a_matrix(jax.random.fold_in(streams_of[3], 71), 0)
    b_matrix = draw_b_matrix(jax.random.fold_in(streams_of[3], 71), 0)
    tile_map = draw_tile_map(jax.random.fold_in(streams_of[3], 71), 0)
    return {"a_matrix": a_matrix, "b_matrix": b_matrix, "tile_map": tile_map}


def reference(a_matrix, b_matrix, tile_map):
    mask = jnp.repeat(jnp.repeat(tile_map, TILE, 0), TILE, 1).astype(jnp.bfloat16)
    masked = a_matrix * mask
    product = jnp.dot(masked, b_matrix, preferred_element_type=jnp.float32)
    diagonal_at = jnp.arange(N, dtype=jnp.int32)
    expanded = product.at[diagonal_at, diagonal_at].add(jnp.float32(N / 32))
    power = expanded * expanded
    column_total = jnp.sum(power, axis=0)
    return jnp.float32(N) * power / column_total[None, :]
```

```python
import functools

import jax
import jax.numpy as jnp
from jax import lax
from jax.experimental import pallas as pl
from jax.experimental.pallas import tpu as pltpu
from jax.sharding import PartitionSpec as P

TILE = 128
CAP = 8
FIRST = 5
SECOND = CAP - FIRST
NZ, NY = 8, 4
RING = (0, -1, 1, -2, 2, -3, 3, -4)
RING_Y = (0, -1, 1, -2)
GROUPS = (RING[:3], RING[3:])


def hop(x, dz, dy):
    pairs = []
    for c in range(2):
        s = 1 - 2 * c
        for z in range(NZ):
            for y in range(NY):
                to = (z + s * dz) % NZ * NY + (y + s * dy) % NY
                pairs.append((c * NZ * NY + z * NY + y, c * NZ * NY + to))
    return lax.ppermute(x, ("col", "layer"), pairs)


def pack_kernel(map_ref, a_ref, p1_ref, p2_ref, idx_ref):
    for s in range(16):
        idx_ref[0, s] = 0

    def step(t, n):
        present = map_ref[t, 0] != 0
        rows = pl.ds(pl.multiple_of(t * TILE, TILE), TILE)

        @pl.when(present)
        def _():
            idx_ref[0, n] = t

        @pl.when(jnp.logical_and(present, n < FIRST))
        def _():
            p1_ref[n] = a_ref[rows, :]

        @pl.when(jnp.logical_and(present, n >= FIRST))
        def _():
            p2_ref[n - FIRST] = a_ref[rows, :]

        return n + present.astype(jnp.int32)

    idx_ref[0, 8] = lax.fori_loop(0, 16, step, jnp.int32(0))


def pack(tile_map, a):
    return pl.pallas_call(
        pack_kernel,
        out_shape=(
            jax.ShapeDtypeStruct((FIRST, TILE, TILE), a.dtype),
            jax.ShapeDtypeStruct((SECOND, TILE, TILE), a.dtype),
            jax.ShapeDtypeStruct((1, 16), jnp.int32),
        ),
        in_specs=[
            pl.BlockSpec(memory_space=pltpu.SMEM),
            pl.BlockSpec(memory_space=pltpu.VMEM),
        ],
        out_specs=(
            pl.BlockSpec(memory_space=pltpu.VMEM),
            pl.BlockSpec(memory_space=pltpu.VMEM),
            pl.BlockSpec(memory_space=pltpu.SMEM),
        ),
    )(tile_map, a)


def product_kernel(plan, idx_ref, b_ref, *refs):
    n = len(plan)
    parts, (keep_ref, send_ref) = refs[:n], refs[n : n + 2]
    slots, sems = refs[n + 2 : 2 * n + 2], refs[2 * n + 2]
    copies = [
        pltpu.make_async_copy(part, slot, sems.at[i])
        for i, (part, slot) in enumerate(zip(parts, slots))
    ]
    for copy in copies:
        copy.start()
    layer = lax.axis_index("layer")
    core = lax.axis_index("col")
    sign = 1 - 2 * core
    z, y = layer // NY, layer % NY
    keep_ref[...] = jnp.zeros_like(keep_ref)
    send_ref[...] = jnp.zeros_like(send_ref)

    for copy, slot, (first, width, sources) in zip(copies, slots, plan):
        copy.wait()
        for j, (dz, dy) in enumerate(sources):
            source = ((z + sign * dz + NZ) % NZ) * NY + (y + sign * dy + NY) % NY
            right = b_ref[pl.ds(pl.multiple_of(source * TILE, TILE), TILE), :]
            here = jnp.clip(idx_ref[source, 8] - first, 0, width)

            def step(i, carry, slot=slot, j=j, source=source, right=right, first=first, width=width):
                t = idx_ref[source, first + i]
                own = (t // 8) == core
                rows = pl.ds(pl.multiple_of((t % 8) * TILE, TILE), TILE)
                term = jnp.dot(
                    slot[j * width + i], right, preferred_element_type=jnp.float32
                )

                @pl.when(own)
                def _():
                    keep_ref[rows, :] += term

                @pl.when(jnp.logical_not(own))
                def _():
                    send_ref[rows, :] += term

                return carry

            lax.fori_loop(0, here, step, 0)


def product(index, b_panel, parts, plan):
    half = (1024, b_panel.shape[1])
    return pl.pallas_call(
        functools.partial(product_kernel, plan),
        out_shape=[jax.ShapeDtypeStruct(half, jnp.float32)] * 2,
        in_specs=[
            pl.BlockSpec(memory_space=pltpu.SMEM),
            pl.BlockSpec(memory_space=pltpu.VMEM),
        ]
        + [pl.BlockSpec(memory_space=pl.ANY)] * len(parts),
        out_specs=[pl.BlockSpec(memory_space=pltpu.VMEM)] * 2,
        scratch_shapes=[pltpu.VMEM(part.shape, part.dtype) for part in parts]
        + [pltpu.SemaphoreType.DMA((len(parts),))],
        compiler_params=pltpu.CompilerParams(vmem_limit_bytes=40 * 1024 * 1024),
    )(index, b_panel, *parts)


def square_kernel(weight, keep_ref, recv_ref, out_ref, sum_ref):
    rows, cols = keep_ref.shape
    first_row = (lax.axis_index("row") * 2 + lax.axis_index("col")) * rows
    first_col = lax.axis_index("layer") * cols
    shape = (TILE, cols)
    total = jnp.zeros((1, cols), jnp.float32)
    for i in range(rows // TILE):
        part = pl.ds(i * TILE, TILE)
        row = lax.broadcasted_iota(jnp.int32, shape, 0) + (first_row + i * TILE)
        col = lax.broadcasted_iota(jnp.int32, shape, 1) + first_col
        diagonal = jnp.where(row == col, jnp.float32(weight), jnp.float32(0))
        expanded = keep_ref[part, :] + recv_ref[part, :] + diagonal
        power = expanded * expanded
        out_ref[part, :] = power
        total += jnp.sum(power, axis=0, keepdims=True)
    sum_ref[...] = total


def square(keep, recv, weight):
    return pl.pallas_call(
        functools.partial(square_kernel, weight),
        out_shape=(
            jax.ShapeDtypeStruct(keep.shape, jnp.float32),
            jax.ShapeDtypeStruct((1, keep.shape[1]), jnp.float32),
        ),
    )(keep, recv)


def scale_kernel(n_total, power_ref, sum_ref, out_ref):
    out_ref[...] = jnp.float32(n_total) * power_ref[...] / sum_ref[...]


def on_device(a_matrix, b_matrix, tile_map):
    n_total = a_matrix.shape[1] * 64
    p1, p2, index = pack(tile_map, a_matrix)
    index = lax.all_gather(index, "layer", axis=0, tiled=True)
    b_panel = lax.all_gather(b_matrix, "row", axis=0, tiled=True)

    back, ahead = hop(p2, 0, 1), hop(p2, 0, -1)
    across = hop(back, 0, 1)
    q = jnp.concatenate([p2, back, ahead, across])
    parts = [q]
    plan = [(FIRST, SECOND, tuple((0, dy) for dy in RING_Y))]
    back = ahead = q
    for k in range(1, 5):
        back = hop(back, 1, 0)
        parts.append(back)
        plan.append((FIRST, SECOND, tuple((-k, dy) for dy in RING_Y)))
        if k < 4:
            ahead = hop(ahead, -1, 0)
            parts.append(ahead)
            plan.append((FIRST, SECOND, tuple((k, dy) for dy in RING_Y)))

    ring = [p1]
    back = ahead = p1
    for k in range(1, 5):
        back = hop(back, 1, 0)
        ring.append(back)
        if k < 4:
            ahead = hop(ahead, -1, 0)
            ring.append(ahead)
    at = 0
    for group in GROUPS:
        g = jnp.concatenate(ring[at : at + len(group)])
        at += len(group)
        back, ahead = hop(g, 0, 1), hop(g, 0, -1)
        across = hop(back, 0, 1)
        for part, dy in zip((g, back, ahead, across), RING_Y):
            parts.append(part)
            plan.append((0, FIRST, tuple((dz, dy) for dz in group)))

    keep, send = product(index, b_panel, parts, tuple(plan))
    recv = lax.ppermute(send, "col", [(0, 1), (1, 0)])
    power, total = square(keep, recv, n_total / 32)
    total = total + lax.ppermute(total, "col", [(0, 1), (1, 0)])
    total = total + lax.ppermute(total, "row", [(i, i ^ 1) for i in range(4)])
    total = total + lax.ppermute(total, "row", [(i, i ^ 2) for i in range(4)])
    return pl.pallas_call(
        functools.partial(scale_kernel, n_total),
        out_shape=jax.ShapeDtypeStruct(power.shape, jnp.float32),
    )(power, total)


def solution(mesh):
    return jax.shard_map(
        on_device,
        mesh=mesh,
        in_specs=(
            P("row", ("col", "layer")),
            P(("col", "row"), "layer"),
            P("row", ("col", "layer")),
        ),
        out_specs=P(("row", "col"), "layer"),
        check_vma=False,
    )
```

```python
import functools

import jax
import jax.numpy as jnp
from jax import lax
from jax.experimental import pallas as pl
from jax.experimental.pallas import tpu as pltpu
from jax.sharding import PartitionSpec as P

TILE = 128
CAP = 8
FIRST = 5
SECOND = CAP - FIRST
HEAD = 16
NZ, NY = 8, 4
RING_Y = (0, -1, 1, -2)
MIB = 1024 * 1024
VMEM = pl.BlockSpec(memory_space=pltpu.VMEM)
SMEM = pl.BlockSpec(memory_space=pltpu.SMEM)


def params(mib):
    return pltpu.CompilerParams(vmem_limit_bytes=mib * MIB)


def hop(x, dz, dy):
    pairs = []
    for c in range(2):
        s = 1 - 2 * c
        for z in range(NZ):
            for y in range(NY):
                to = (z + s * dz) % NZ * NY + (y + s * dy) % NY
                pairs.append((c * NZ * NY + z * NY + y, c * NZ * NY + to))
    return lax.ppermute(x, ("col", "layer"), pairs)


class Line:
    def __init__(self, depth):
        self.depth = depth
        self.done = []

    def __call__(self, x, dz, dy):
        if len(self.done) >= self.depth:
            x, _ = lax.optimization_barrier((x, self.done[-self.depth]))
        out = hop(x, dz, dy)
        self.done.append(out)
        return out


def pack_kernel(map_ref, a_ref, p1_ref, p2_ref):
    lane = lax.broadcasted_iota(jnp.int32, (HEAD, TILE), 1)

    def step(t, carry):
        n, head = carry
        present = map_ref[0, t] != 0
        rows = pl.ds(pl.multiple_of(t * TILE, TILE), TILE)

        @pl.when(jnp.logical_and(present, n < FIRST))
        def _():
            p1_ref[0, pl.ds(pl.multiple_of(n * TILE, TILE), TILE), :] = a_ref[rows, :]

        @pl.when(jnp.logical_and(present, n >= FIRST))
        def _():
            p2_ref[0, pl.ds(pl.multiple_of((n - FIRST) * TILE, TILE), TILE), :] = a_ref[rows, :]

        head = jnp.where(jnp.logical_and(lane == n, present), t.astype(jnp.float32), head)
        return n + present.astype(jnp.int32), head

    count, head = lax.fori_loop(
        0, 16, step, (jnp.int32(0), jnp.zeros((HEAD, TILE), jnp.float32))
    )
    head = jnp.where(lane == CAP, count.astype(jnp.float32), head).astype(p1_ref.dtype)
    p1_ref[0, FIRST * TILE :, :] = head
    p2_ref[0, SECOND * TILE :, :] = head


def pack(tile_map, a):
    return pl.pallas_call(
        pack_kernel,
        out_shape=[
            jax.ShapeDtypeStruct((1, n * TILE + HEAD, TILE), a.dtype) for n in (FIRST, SECOND)
        ],
        in_specs=[SMEM, VMEM],
        out_specs=[VMEM, VMEM],
        compiler_params=params(4),
    )(tile_map, a)


def join_kernel(*refs):
    out_ref = refs[-1]
    for i, ref in enumerate(refs[:-1]):
        out_ref[i] = ref[0]


def join(parts):
    shape = (len(parts),) + parts[0].shape[1:]
    return pl.pallas_call(
        join_kernel,
        out_shape=jax.ShapeDtypeStruct(shape, parts[0].dtype),
        in_specs=[VMEM] * len(parts),
        out_specs=VMEM,
        compiler_params=params(4),
    )(*parts)


def product_kernel(plan, fresh, last, *refs):
    n = len(plan)
    b_ref, parts, refs = refs[0], refs[1 : n + 1], refs[n + 1 :]
    if not fresh:
        refs = refs[1:]
    if last:
        keep_ref, send_ref, total_ref, heads_ref, table_ref, sem = refs
    else:
        total_ref, heads_ref, table_ref, sem = refs
    at = 0
    for part, (first, width, sources) in zip(parts, plan):
        for j in range(len(sources)):
            head = part[j, width * TILE : width * TILE + HEAD, :].astype(jnp.float32)
            heads_ref[at : at + 1, :] = head[0:1, :].astype(jnp.int32)
            at += 1
    copy = pltpu.make_async_copy(heads_ref, table_ref, sem)
    copy.start()
    if fresh:
        total_ref[...] = jnp.zeros_like(total_ref)
    layer = lax.axis_index("layer")
    core = lax.axis_index("col")
    sign = 1 - 2 * core
    z, y = layer // NY, layer % NY
    copy.wait()

    at = 0
    for part, (first, width, sources) in zip(parts, plan):
        for j, (dz, dy) in enumerate(sources):
            source = ((z + sign * dz + NZ) % NZ) * NY + (y + sign * dy + NY) % NY
            start = pl.multiple_of(source * TILE, TILE)
            count = jnp.clip(table_ref[at, CAP] - first, 0, width)

            for m in range(1, width + 1):

                @pl.when(count == m)
                def _(m=m, j=j, at=at, part=part, first=first, start=start):
                    term = jnp.dot(
                        part[j, : m * TILE, :],
                        b_ref[pl.ds(start, TILE), :],
                        preferred_element_type=jnp.float32,
                    )
                    for i in range(m):
                        t = table_ref[at, first + i]
                        t = jnp.where(core == 0, t, (t + 8) % 16)
                        rows = pl.ds(pl.multiple_of(t * TILE, TILE), TILE)
                        total_ref[rows, :] += term[i * TILE : (i + 1) * TILE, :]

            at += 1
    if last:
        half = keep_ref.shape[0]
        keep_ref[...] = total_ref[:half, :]
        send_ref[...] = total_ref[half:, :]


def product(b_panel, parts, plan, total=None, last=False):
    cols = b_panel.shape[1]
    whole = jax.ShapeDtypeStruct((2048, cols), jnp.float32)
    half = jax.ShapeDtypeStruct((1024, cols), jnp.float32)
    count = sum(len(sources) for _, _, sources in plan)
    count = (count + 7) // 8 * 8
    operands = [b_panel, *parts] + ([] if total is None else [total])
    scratch = [
        pltpu.VMEM((count, TILE), jnp.int32),
        pltpu.SMEM((count, TILE), jnp.int32),
        pltpu.SemaphoreType.DMA(()),
    ]
    alias = {} if total is None else {len(operands) - 1: 2 if last else 0}
    outs = [half, half, whole] if last else [whole]
    size = sum(p.size for p in parts)
    return pl.pallas_call(
        functools.partial(product_kernel, tuple(plan), total is None, last),
        out_shape=outs,
        in_specs=[VMEM] * len(operands),
        out_specs=[VMEM] * len(outs),
        scratch_shapes=scratch,
        input_output_aliases=alias,
        compiler_params=params(24),
        cost_estimate=pl.CostEstimate(
            flops=size * cols * 2, bytes_accessed=size * 4, transcendentals=0
        ),
    )(*operands)


def expand(weight, keep_ref, recv_ref, i):
    rows, cols = keep_ref.shape
    first_row = (lax.axis_index("row") * 2 + lax.axis_index("col")) * rows + i * TILE
    first_col = lax.axis_index("layer") * cols
    shape = (TILE, cols)
    part = pl.ds(i * TILE, TILE)
    row = lax.broadcasted_iota(jnp.int32, shape, 0) + (first_row - first_col)
    col = lax.broadcasted_iota(jnp.int32, shape, 1)
    diagonal = jnp.where(row == col, jnp.float32(weight), jnp.float32(0))
    return keep_ref[part, :] + recv_ref[part, :] + diagonal


def square_kernel(weight, keep_ref, recv_ref, out_ref, sum_ref):
    rows, cols = keep_ref.shape
    total = jnp.zeros((TILE, cols), jnp.float32)
    for i in range(rows // TILE):
        expanded = expand(weight, keep_ref, recv_ref, i)
        power = expanded * expanded
        out_ref[pl.ds(i * TILE, TILE), :] = power
        total += power
    sum_ref[...] = jnp.sum(total, axis=0, keepdims=True)


def square(keep, recv, weight):
    return pl.pallas_call(
        functools.partial(square_kernel, weight),
        out_shape=(
            jax.ShapeDtypeStruct(keep.shape, jnp.float32),
            jax.ShapeDtypeStruct((1, keep.shape[1]), jnp.float32),
        ),
        in_specs=[VMEM] * 2,
        out_specs=[VMEM] * 2,
        compiler_params=params(8),
    )(keep, recv)


def scale_kernel(n_total, power_ref, *refs):
    out_ref = refs[-1]
    total = sum(ref[...] for ref in refs[1:-1]) + refs[0][...]
    out_ref[...] = jnp.float32(n_total) * power_ref[...] / total


def on_device(a_matrix, b_matrix, tile_map):
    n_total = a_matrix.shape[1] * 64
    p1, p2 = pack(tile_map.reshape(1, 16), a_matrix)
    b_panel = lax.all_gather(b_matrix, "row", axis=0, tiled=True)
    along_z, along_y = Line(3), Line(2)

    a1, b1 = along_z(p1, 1, 0), along_z(p1, -1, 0)
    back, ahead = along_y(p2, 0, 1), along_y(p2, 0, -1)
    across = along_y(back, 0, 1)
    a2, b2 = along_z(a1, 1, 0), along_z(b1, -1, 0)
    g1 = join([p1, a1, b1])
    g1_back, g1_ahead = along_y(g1, 0, 1), along_y(g1, 0, -1)
    q = join([p2, back, ahead, across])
    qa1 = along_z(q, 1, 0)
    a3, b3 = along_z(a2, 1, 0), along_z(b2, -1, 0)
    qb1 = along_z(q, -1, 0)
    a4 = along_z(a3, 1, 0)
    g1_across = along_y(g1_back, 0, 1)
    g2 = join([a2, b2, a3, b3, a4])
    g2_back, g2_ahead = along_y(g2, 0, 1), along_y(g2, 0, -1)
    qa2 = along_z(qa1, 1, 0)
    qb2 = along_z(qb1, -1, 0)
    qa3 = along_z(qa2, 1, 0)
    qb3 = along_z(qb2, -1, 0)

    def slots_first(group):
        return [(0, FIRST, tuple((dz, dy) for dz in group)) for dy in RING_Y]

    def slots_second(dz):
        return (FIRST, SECOND, tuple((dz, dy) for dy in RING_Y))

    near, far = slots_first((0, -1, 1)), slots_first((-2, 2, -3, 3, -4))
    (total,) = product(
        b_panel,
        [g1, g1_back, g1_ahead, g1_across, g2, q, qa1, qb1],
        near + far[:1] + [slots_second(dz) for dz in (0, -1, 1)],
    )
    qa3, total = lax.optimization_barrier((qa3, total))
    qa4 = along_z(qa3, 1, 0)
    g2_across = along_y(g2_back, 0, 1)
    (total,) = product(
        b_panel,
        [g2_back, qa2, qb2, qa3, qb3],
        far[1:2] + [slots_second(dz) for dz in (-2, 2, -3, 3)],
        total,
    )
    keep, send, _ = product(
        b_panel,
        [g2_ahead, g2_across, qa4],
        far[2:] + [slots_second(-4)],
        total,
        last=True,
    )
    recv = lax.ppermute(send, "col", [(0, 1), (1, 0)])
    power, total = square(keep, recv, n_total / 32)
    total = total + lax.ppermute(total, "col", [(0, 1), (1, 0)])
    others = [
        lax.ppermute(total, "row", [(i, (i + d) % 4) for i in range(4)]) for d in (1, 3, 2)
    ]
    return pl.pallas_call(
        functools.partial(scale_kernel, n_total),
        out_shape=jax.ShapeDtypeStruct(power.shape, jnp.float32),
        in_specs=[VMEM] * 5,
        out_specs=VMEM,
        compiler_params=params(8),
    )(power, total, *others)


def solution(mesh):
    return jax.shard_map(
        on_device,
        mesh=mesh,
        in_specs=(
            P("row", ("col", "layer")),
            P(("col", "row"), "layer"),
            P("row", ("col", "layer")),
        ),
        out_specs=P(("row", "col"), "layer"),
        check_vma=False,
    )
```

```python
import functools

import jax
import jax.numpy as jnp
from jax import lax
from jax.experimental import pallas as pl
from jax.experimental.pallas import tpu as pltpu
from jax.sharding import PartitionSpec as P

TILE = 128
CAP = 8
HEAD = 16
SLAB = CAP * TILE + HEAD
NX, NY, NZ = 4, 4, 8
ROWS = 2048
LEVELS = 65535
FINE = 64
BATCH = 4
MIB = 1024 * 1024
VMEM = pl.BlockSpec(memory_space=pltpu.VMEM)
SMEM = pl.BlockSpec(memory_space=pltpu.SMEM)


def struct(shape, dtype):
    return jax.ShapeDtypeStruct(shape, dtype)


def call(kernel, out_shape, *operands, first=VMEM, mib=8, **kwargs):
    many = isinstance(out_shape, (list, tuple))
    return pl.pallas_call(
        kernel,
        out_shape=out_shape,
        in_specs=[first] + [VMEM] * (len(operands) - 1),
        out_specs=[VMEM] * len(out_shape) if many else VMEM,
        compiler_params=pltpu.CompilerParams(vmem_limit_bytes=mib * MIB),
        **kwargs,
    )(*operands)


def after(x, *others):
    return lax.optimization_barrier((x, *others))[0]


def hop(x, dz, dy):
    pairs = []
    for c in range(2):
        s = 1 - 2 * c
        for z in range(NZ):
            for y in range(NY):
                to = (z + s * dz) % NZ * NY + (y + s * dy) % NY
                pairs.append((c * NZ * NY + z * NY + y, c * NZ * NY + to))
    return lax.ppermute(x, ("col", "layer"), pairs)


def hop_x(x, dx):
    pairs = []
    for c in range(2):
        s = 1 - 2 * c
        pairs += [(i * 2 + c, (i + s * dx) % NX * 2 + c) for i in range(NX)]
    return lax.ppermute(x, ("row", "col"), pairs)


def swap(x):
    return lax.ppermute(x, "col", [(0, 1), (1, 0)])


def place():
    layer, core = lax.axis_index("layer"), lax.axis_index("col")
    return layer // NY, layer % NY, core, 1 - 2 * core


def pack_kernel(map_ref, a_ref, out_ref):
    lane = lax.broadcasted_iota(jnp.int32, (HEAD, TILE), 1)

    def step(t, carry):
        n, head = carry
        present = map_ref[0, t] != 0

        @pl.when(jnp.logical_and(present, n < CAP))
        def _():
            rows = pl.ds(pl.multiple_of(t * TILE, TILE), TILE)
            out_ref[pl.ds(pl.multiple_of(n * TILE, TILE), TILE), :] = a_ref[rows, :]

        head = jnp.where(jnp.logical_and(lane == n, present), t.astype(jnp.float32), head)
        return n + present.astype(jnp.int32), head

    count, head = lax.fori_loop(
        0, 16, step, (jnp.int32(0), jnp.zeros((HEAD, TILE), jnp.float32))
    )
    head = jnp.where(lane == CAP, count.astype(jnp.float32), head)
    out_ref[CAP * TILE :, :] = head.astype(out_ref.dtype)


def split_kernel(b_ref, keep_ref, send_ref):
    core = lax.axis_index("col")
    left, right = b_ref[:, :TILE], b_ref[:, TILE:]
    keep_ref[...] = jnp.where(core == 0, left, right)
    send_ref[...] = jnp.where(core == 0, right, left)


def block_kernel(keep_ref, recv_ref, *out_refs):
    _, y, _, s = place()
    for d, out_ref in zip((0, 1, -1, 2), out_refs):
        to = (y + s * d + NY) % NY
        for r, ref in enumerate((keep_ref, recv_ref)):
            for low in range(2):
                rows = pl.ds(pl.multiple_of((low * NY + to) * TILE, TILE), TILE)
                at = (r * 2 + low) * TILE
                out_ref[at : at + TILE, :] = ref[rows, :]


def widen_kernel(*refs):
    for i, ref in enumerate(refs[:-1]):
        refs[-1][:, i * TILE : (i + 1) * TILE] = ref[...]


def stack_kernel(own_ref, far_ref, back_ref, ahead_ref, out_ref):
    x, s = lax.axis_index("row"), 1 - 2 * lax.axis_index("col")
    for d, ref in ((0, own_ref), (-1, back_ref), (1, ahead_ref), (2, far_ref)):
        out_ref[(x + s * d + NX) % NX] = ref[...]


def join_kernel(*refs):
    for i, ref in enumerate(refs[:-1]):
        refs[-1][i] = ref[...]


def join(parts):
    return call(join_kernel, struct((len(parts), *parts[0].shape), parts[0].dtype), *parts)


def product_kernel(plan, *refs):
    n = len(plan)
    b_ref, parts = refs[0], refs[1 : n + 1]
    total_ref, heads_ref, table_ref, work_ref, sem = refs[n + 1 :]
    at = 0
    for part, (_, steps) in zip(parts, plan):
        for j in range(len(steps)):
            head = part[j, CAP * TILE :, :].astype(jnp.float32)
            heads_ref[at : at + 1, :] = head[0:1, :].astype(jnp.int32)
            at += 1
    copy = pltpu.make_async_copy(heads_ref, table_ref, sem)
    copy.start()
    total_ref[...] = jnp.zeros_like(total_ref)
    z, _, _, s = place()
    copy.wait()

    at = 0
    for part, (other, steps) in zip(parts, plan):
        count = jnp.int32(0)
        for j, dz in enumerate(steps):
            source = (z + (-s if other else s) * dz + NZ) % NZ

            def list_tile(i, count, j=j, at=at, source=source, other=other):
                work_ref[0, count] = j
                work_ref[1, count] = i
                work_ref[2, count] = table_ref[at, i]
                work_ref[3, count] = source // 2
                work_ref[4, count] = other * 2 + source % 2
                return count + 1

            count = lax.fori_loop(0, table_ref[at, CAP], list_tile, count)
            at += 1
        for u in range(BATCH - 1):
            for k, v in enumerate((0, 0, ROWS // TILE, 0, 0)):
                work_ref[k, count + u] = v

        def step(g, carry, part=part):
            for u in range(BATCH):
                j, i, t, panel, at_b = (work_ref[k, g * BATCH + u] for k in range(5))
                rows = pl.ds(pl.multiple_of(t * TILE, TILE), TILE)
                total_ref[rows, :] += jnp.dot(
                    part[j, pl.ds(pl.multiple_of(i * TILE, TILE), TILE), :],
                    b_ref[panel, pl.ds(pl.multiple_of(at_b * TILE, TILE), TILE), :],
                    preferred_element_type=jnp.float32,
                )
            return carry

        lax.fori_loop(0, (count + BATCH - 1) // BATCH, step, 0)


def product(b_panel, parts, plan):
    cols = b_panel.shape[2]
    count = sum(len(steps) for _, steps in plan)
    flops = sum(p.size for p in parts) * cols * 2
    return call(
        functools.partial(product_kernel, tuple(plan)),
        struct((ROWS + TILE, cols), jnp.float32),
        b_panel,
        *parts,
        mib=20,
        scratch_shapes=[
            pltpu.VMEM((count, TILE), jnp.int32),
            pltpu.SMEM((count, TILE), jnp.int32),
            pltpu.SMEM((8, TILE), jnp.int32),
            pltpu.SemaphoreType.DMA(()),
        ],
        cost_estimate=pl.CostEstimate(flops=flops, bytes_accessed=flops // 128, transcendentals=0),
    )


def encode_kernel(slot, total_ref, out_ref):
    lanes = slice(slot * TILE, (slot + 1) * TILE)
    top = total_ref[:TILE, lanes]
    for i in range(1, ROWS // TILE):
        top = jnp.maximum(top, total_ref[i * TILE : (i + 1) * TILE, lanes])
    top = jnp.maximum(jnp.max(top, axis=0, keepdims=True), jnp.float32(2.0**-100))
    exponent = jnp.ceil(jnp.log2(top) * FINE)
    inverse = LEVELS * jnp.exp2(exponent * (-1.0 / FINE))
    for i in range(ROWS // TILE):
        part = slice(i * TILE, (i + 1) * TILE)
        steps = jnp.minimum(total_ref[part, lanes] * inverse + 0.5, jnp.float32(LEVELS))
        out_ref[part, :] = (steps.astype(jnp.int32) - 32768).astype(jnp.int16)
    exponent = jnp.broadcast_to(exponent, (HEAD, TILE)).astype(jnp.int32)
    out_ref[ROWS:, :] = exponent.astype(jnp.int16)


def encode(total, slot):
    return call(
        functools.partial(encode_kernel, slot), struct((ROWS + HEAD, TILE), jnp.int16), total
    )


def square_kernel(weight, total_ref, *refs):
    recv, (keep_ref, send_ref, sum_ref) = refs[:3], refs[3:]
    core = lax.axis_index("col")
    first_col = lax.axis_index("layer") * 2 * TILE + core * TILE
    scales = []
    for ref in recv:
        exponent = ref[ROWS:, :].astype(jnp.int32).astype(jnp.float32)[0:1, :]
        scales.append(jnp.exp2(exponent * (1.0 / FINE)) * jnp.float32(1.0 / LEVELS))
    row = lax.broadcasted_iota(jnp.int32, (TILE, TILE), 0)
    col = lax.broadcasted_iota(jnp.int32, (TILE, TILE), 1)
    column = jnp.zeros((TILE, TILE), jnp.float32)
    half = ROWS // 2
    for i in range(half // TILE):
        for own, out_ref in ((1, keep_ref), (0, send_ref)):
            start = (core if own else 1 - core) * half + i * TILE
            part = pl.ds(pl.multiple_of(start, TILE), TILE)
            first_row = lax.axis_index("row") * ROWS + start
            diagonal = row + (first_row - first_col) == col
            expanded = total_ref[part, :TILE] + jnp.where(
                diagonal, jnp.float32(weight), jnp.float32(0)
            )
            for ref, scale in zip(recv, scales):
                steps = ref[part, :].astype(jnp.int32) + 32768
                expanded += steps.astype(jnp.float32) * scale
            power = expanded * expanded
            out_ref[i * TILE : (i + 1) * TILE, :] = power
            column += power
    sum_ref[...] = jnp.sum(column, axis=0, keepdims=True)


def scale_kernel(n_total, keep_ref, recv_ref, *refs):
    out_ref = refs[-1]
    total = refs[0][...]
    for ref in refs[1:-1]:
        total += ref[...]
    core = lax.axis_index("col")
    own = jnp.float32(n_total) * keep_ref[...] / total[0:1, :]
    other = jnp.float32(n_total) * recv_ref[...] / total[1:2, :]
    out_ref[:, :TILE] = jnp.where(core == 0, own, other)
    out_ref[:, TILE:] = jnp.where(core == 0, other, own)


def on_device(a_matrix, b_matrix, tile_map):
    n_total = a_matrix.shape[1] * 64
    half = ROWS // 2
    keep, send = call(split_kernel, [struct((half, TILE), b_matrix.dtype)] * 2, b_matrix)
    recv = swap(send)
    p = call(
        pack_kernel,
        struct((SLAB, TILE), a_matrix.dtype),
        tile_map.reshape(1, 16),
        a_matrix,
        first=SMEM,
    )
    a1, b1 = hop(p, 1, 0), hop(p, -1, 0)
    blocks = call(block_kernel, [struct((512, TILE), b_matrix.dtype)] * 4, keep, recv)
    blocks = [blocks[0]] + [hop(m, 0, d) for m, d in zip(blocks[1:], (1, -1, 2))]
    wide = call(widen_kernel, struct((512, 4 * TILE), b_matrix.dtype), *blocks)

    a1, b1 = after(a1, wide), after(b1, wide)
    a2, b2 = hop(a1, 1, 0), hop(b1, -1, 0)
    back, ahead = hop_x(wide, 1), hop_x(wide, -1)
    near = join([p, a1, b1, a2, b2])
    a2, b2 = after(a2, back), after(b2, back)
    a4, a3, b3 = hop(a2, 2, 0), hop(a2, 1, 0), hop(b2, -1, 0)
    across = hop_x(back, 1)
    near_other = swap(near)
    far = join([after(a3, across, ahead), b3, a4])
    far_other = swap(far)
    panel = call(
        stack_kernel, struct((NX, 512, 4 * TILE), b_matrix.dtype), wide, across, back, ahead
    )
    near_steps, far_steps = (0, -1, 1, -2, 2), (-3, 3, -4)
    total = product(
        panel,
        [near, near_other, far, far_other],
        [(0, near_steps), (1, near_steps), (0, far_steps), (1, far_steps)],
    )

    sums = [hop(encode(total, slot), 0, d) for slot, d in ((3, 2), (1, -1), (2, 1))]
    keep, send, column = call(
        functools.partial(square_kernel, n_total / 32),
        [struct((half, TILE), jnp.float32)] * 2 + [struct((1, TILE), jnp.float32)],
        total,
        *sums,
    )
    column = jnp.concatenate([column, swap(column)])
    recv = swap(send)
    columns = [column] + [hop_x(column, d) for d in (1, -1, 2)]
    return call(
        functools.partial(scale_kernel, n_total),
        struct((half, 2 * TILE), jnp.float32),
        keep,
        recv,
        *columns,
    )


def solution(mesh):
    return jax.shard_map(
        on_device,
        mesh=mesh,
        in_specs=(
            P("row", ("col", "layer")),
            P(("col", "row"), "layer"),
            P("row", ("col", "layer")),
        ),
        out_specs=P(("row", "col"), "layer"),
        check_vma=False,
    )
```

```python
import functools

import jax
import jax.numpy as jnp
from jax import lax
from jax.experimental import pallas as pl
from jax.experimental.pallas import tpu as pltpu
from jax.sharding import PartitionSpec as P

TILE = 128
CAP = 8
HEAD = 16
SLAB = CAP * TILE + HEAD
NX, NY, NZ = 4, 4, 8
ROWS = 2048
LEVELS = 65535
FINE = 64
BATCH = 4
MIB = 1024 * 1024
VMEM = pl.BlockSpec(memory_space=pltpu.VMEM)
SMEM = pl.BlockSpec(memory_space=pltpu.SMEM)


def struct(shape, dtype):
    return jax.ShapeDtypeStruct(shape, dtype)


def call(kernel, out_shape, *operands, first=VMEM, mib=8, **kwargs):
    many = isinstance(out_shape, (list, tuple))
    return pl.pallas_call(
        kernel,
        out_shape=out_shape,
        in_specs=[first] + [VMEM] * (len(operands) - 1),
        out_specs=[VMEM] * len(out_shape) if many else VMEM,
        compiler_params=pltpu.CompilerParams(vmem_limit_bytes=mib * MIB),
        **kwargs,
    )(*operands)


def after(x, *others):
    return lax.optimization_barrier((x, *others))[0]


def hop(x, dz, dy):
    pairs = []
    for c in range(2):
        s = 1 - 2 * c
        for z in range(NZ):
            for y in range(NY):
                to = (z + s * dz) % NZ * NY + (y + s * dy) % NY
                pairs.append((c * NZ * NY + z * NY + y, c * NZ * NY + to))
    return lax.ppermute(x, ("col", "layer"), pairs)


def hop_x(x, dx):
    pairs = []
    for c in range(2):
        s = 1 - 2 * c
        pairs += [(i * 2 + c, (i + s * dx) % NX * 2 + c) for i in range(NX)]
    return lax.ppermute(x, ("row", "col"), pairs)


def swap(x):
    return lax.ppermute(x, "col", [(0, 1), (1, 0)])


def place():
    layer, core = lax.axis_index("layer"), lax.axis_index("col")
    return layer // NY, layer % NY, core, 1 - 2 * core


def pack_kernel(map_ref, a_ref, out_ref):
    lane = lax.broadcasted_iota(jnp.int32, (HEAD, TILE), 1)

    def step(t, carry):
        n, head = carry
        present = map_ref[0, t] != 0

        @pl.when(jnp.logical_and(present, n < CAP))
        def _():
            rows = pl.ds(pl.multiple_of(t * TILE, TILE), TILE)
            out_ref[pl.ds(pl.multiple_of(n * TILE, TILE), TILE), :] = a_ref[rows, :]

        head = jnp.where(jnp.logical_and(lane == n, present), t.astype(jnp.float32), head)
        return n + present.astype(jnp.int32), head

    count, head = lax.fori_loop(
        0, 16, step, (jnp.int32(0), jnp.zeros((HEAD, TILE), jnp.float32))
    )
    head = jnp.where(lane == CAP, count.astype(jnp.float32), head)
    out_ref[CAP * TILE :, :] = head.astype(out_ref.dtype)


def split_kernel(b_ref, keep_ref, send_ref):
    core = lax.axis_index("col")
    left, right = b_ref[:, :TILE], b_ref[:, TILE:]
    keep_ref[...] = jnp.where(core == 0, left, right)
    send_ref[...] = jnp.where(core == 0, right, left)


def block_kernel(keep_ref, recv_ref, *out_refs):
    _, y, _, s = place()
    for d, out_ref in zip((0, 1, -1, 2), out_refs):
        to = (y + s * d + NY) % NY
        for r, ref in enumerate((keep_ref, recv_ref)):
            for low in range(2):
                rows = pl.ds(pl.multiple_of((low * NY + to) * TILE, TILE), TILE)
                at = (r * 2 + low) * TILE
                out_ref[at : at + TILE, :] = ref[rows, :]


def widen_kernel(*refs):
    for i, ref in enumerate(refs[:-1]):
        refs[-1][:, i * TILE : (i + 1) * TILE] = ref[...]


def stack_kernel(places, *refs):
    out_ref = refs[-1]
    for place, ref in zip(places, refs):
        out_ref[place] = ref[...]


def stack(panels, places, whole=None):
    out = struct((NX, *panels[0].shape), panels[0].dtype)
    operands = panels + ([] if whole is None else [whole])
    alias = {} if whole is None else {len(panels): 0}
    return call(functools.partial(stack_kernel, places), out, *operands, input_output_aliases=alias)


def join_kernel(*refs):
    for i, ref in enumerate(refs[:-1]):
        refs[-1][i] = ref[...]


def join(parts):
    return call(join_kernel, struct((len(parts), *parts[0].shape), parts[0].dtype), *parts)


def product_kernel(plan, slots, outs, *refs):
    n = len(plan)
    b_ref, parts, given = refs[0], refs[1 : n + 1], refs[n + 1 : -5 - len(outs)]
    out_refs = refs[-5 - len(outs) : -5]
    total_ref, heads_ref, table_ref, work_ref, sem = refs[-5:]
    at = 0
    for part, (_, _, steps) in zip(parts, plan):
        for j in range(len(steps)):
            head = part[j, CAP * TILE :, :].astype(jnp.float32)
            heads_ref[at : at + 1, :] = head[0:1, :].astype(jnp.int32)
            at += 1
    copy = pltpu.make_async_copy(heads_ref, table_ref, sem)
    copy.start()
    lanes = slice(slots[0] * TILE, (slots[-1] + 1) * TILE)
    if given:
        total_ref[...] = given[0][:, lanes]
    else:
        total_ref[...] = jnp.zeros_like(total_ref)
    z, _, _, s = place()
    x = lax.axis_index("row")
    copy.wait()

    at = 0
    for part, (other, panels, steps) in zip(parts, plan):
        count = jnp.int32(0)
        for j, dz in enumerate(steps):
            source = (z + (-s if other else s) * dz + NZ) % NZ
            panel = ((source // 2 - x) * s + NX) % NX
            tiles = table_ref[at, CAP]
            if len(panels) < NX:
                held = functools.reduce(jnp.logical_or, [panel == k for k in panels])
                tiles = jnp.where(held, tiles, 0)

            def list_tile(i, count, j=j, at=at, source=source, other=other, panel=panel):
                work_ref[0, count] = j
                work_ref[1, count] = i
                work_ref[2, count] = table_ref[at, i]
                work_ref[3, count] = panel
                work_ref[4, count] = other * 2 + source % 2
                return count + 1

            count = lax.fori_loop(0, tiles, list_tile, count)
            at += 1
        for u in range(BATCH - 1):
            for k, v in enumerate((0, 0, ROWS // TILE, panels[0], 0)):
                work_ref[k, count + u] = v

        def step(g, carry, part=part):
            for u in range(BATCH):
                j, i, t, panel, at_b = (work_ref[k, g * BATCH + u] for k in range(5))
                rows = pl.ds(pl.multiple_of(t * TILE, TILE), TILE)
                total_ref[rows, :] += jnp.dot(
                    part[j, pl.ds(pl.multiple_of(i * TILE, TILE), TILE), :],
                    b_ref[panel, pl.ds(pl.multiple_of(at_b * TILE, TILE), TILE), lanes],
                    preferred_element_type=jnp.float32,
                )
            return carry

        lax.fori_loop(0, (count + BATCH - 1) // BATCH, step, 0)
    for i, (coded, out_ref) in enumerate(zip(outs, out_refs)):
        part = slice(i * TILE, (i + 1) * TILE)
        if coded:
            encode(total_ref, part, out_ref)
        elif len(outs) == 1:
            out_ref[...] = total_ref[...]
        else:
            out_ref[...] = total_ref[:, part]


def product(b_panels, parts, plan, total=None, slots=(0, 1, 2, 3), outs=(False,)):
    cols = len(slots) * TILE
    count = sum(len(steps) for _, _, steps in plan)
    flops = sum(p.size for p in parts) * cols * 2
    width = cols // len(outs)
    return call(
        functools.partial(product_kernel, tuple(plan), slots, outs),
        [
            struct((ROWS + HEAD, TILE), jnp.int16)
            if coded
            else struct((ROWS + TILE, width), jnp.float32)
            for coded in outs
        ],
        b_panels,
        *parts,
        *([] if total is None else [total]),
        mib=24,
        scratch_shapes=[
            pltpu.VMEM((ROWS + TILE, cols), jnp.float32),
            pltpu.VMEM((count, TILE), jnp.int32),
            pltpu.SMEM((count, TILE), jnp.int32),
            pltpu.SMEM((8, TILE), jnp.int32),
            pltpu.SemaphoreType.DMA(()),
        ],
        cost_estimate=pl.CostEstimate(flops=flops, bytes_accessed=flops // 128, transcendentals=0),
    )


def encode(total_ref, lanes, out_ref):
    top = total_ref[:TILE, lanes]
    for i in range(1, ROWS // TILE):
        top = jnp.maximum(top, total_ref[i * TILE : (i + 1) * TILE, lanes])
    top = jnp.maximum(jnp.max(top, axis=0, keepdims=True), jnp.float32(2.0**-100))
    exponent = jnp.ceil(jnp.log2(top) * FINE)
    inverse = LEVELS * jnp.exp2(exponent * (-1.0 / FINE))
    for i in range(ROWS // TILE):
        part = slice(i * TILE, (i + 1) * TILE)
        steps = jnp.minimum(total_ref[part, lanes] * inverse + 0.5, jnp.float32(LEVELS))
        out_ref[part, :] = (steps.astype(jnp.int32) - 32768).astype(jnp.int16)
    exponent = jnp.broadcast_to(exponent, (HEAD, TILE)).astype(jnp.int32)
    out_ref[ROWS:, :] = exponent.astype(jnp.int16)


def scale_of(ref):
    exponent = ref[ROWS:, :].astype(jnp.int32).astype(jnp.float32)[0:1, :]
    return jnp.exp2(exponent * (1.0 / FINE)) * jnp.float32(1.0 / LEVELS)


def decode(ref, part, scale):
    return (ref[part, :].astype(jnp.int32) + 32768).astype(jnp.float32) * scale


def relay_kernel(total_ref, recv_ref, out_ref, sum_ref):
    scale = scale_of(recv_ref)
    for i in range(ROWS // TILE):
        part = slice(i * TILE, (i + 1) * TILE)
        sum_ref[part, :] = total_ref[part, :] + decode(recv_ref, part, scale)
    encode(sum_ref, slice(0, TILE), out_ref)


def square_kernel(weight, total_ref, *refs):
    recv, (keep_ref, send_ref, sum_ref) = refs[:2], refs[2:]
    core = lax.axis_index("col")
    first_col = lax.axis_index("layer") * 2 * TILE + core * TILE
    scales = [scale_of(ref) for ref in recv]
    row = lax.broadcasted_iota(jnp.int32, (TILE, TILE), 0)
    col = lax.broadcasted_iota(jnp.int32, (TILE, TILE), 1)
    column = jnp.zeros((TILE, TILE), jnp.float32)
    half = ROWS // 2
    for i in range(half // TILE):
        for own, out_ref in ((1, keep_ref), (0, send_ref)):
            start = (core if own else 1 - core) * half + i * TILE
            part = pl.ds(pl.multiple_of(start, TILE), TILE)
            first_row = lax.axis_index("row") * ROWS + start
            diagonal = row + (first_row - first_col) == col
            expanded = total_ref[part, :] + jnp.where(
                diagonal, jnp.float32(weight), jnp.float32(0)
            )
            for ref, scale in zip(recv, scales):
                expanded += decode(ref, part, scale)
            power = expanded * expanded
            out_ref[i * TILE : (i + 1) * TILE, :] = power
            column += power
    sum_ref[...] = jnp.sum(column, axis=0, keepdims=True)


def scale_kernel(n_total, keep_ref, recv_ref, *refs):
    out_ref = refs[-1]
    total = refs[0][...]
    for ref in refs[1:-1]:
        total += ref[...]
    core = lax.axis_index("col")
    own = jnp.float32(n_total) * keep_ref[...] / total[0:1, :]
    other = jnp.float32(n_total) * recv_ref[...] / total[1:2, :]
    out_ref[:, :TILE] = jnp.where(core == 0, own, other)
    out_ref[:, TILE:] = jnp.where(core == 0, other, own)


def on_device(a_matrix, b_matrix, tile_map):
    n_total = a_matrix.shape[1] * 64
    half = ROWS // 2
    keep, send = call(split_kernel, [struct((half, TILE), b_matrix.dtype)] * 2, b_matrix)
    recv = swap(send)
    p = call(
        pack_kernel,
        struct((SLAB, TILE), a_matrix.dtype),
        tile_map.reshape(1, 16),
        a_matrix,
        first=SMEM,
    )
    a1, b1 = hop(p, 1, 0), hop(p, -1, 0)
    blocks = call(block_kernel, [struct((512, TILE), b_matrix.dtype)] * 4, after(keep, p), recv)
    blocks = [blocks[0]] + [hop(m, 0, d) for m, d in zip(blocks[1:], (1, -1, 2))]
    wide = call(widen_kernel, struct((512, 4 * TILE), b_matrix.dtype), *blocks)

    a1, b1 = after(a1, wide), after(b1, wide)
    a2, b2, a4 = hop(a1, 1, 0), hop(b1, -1, 0), hop(a1, 3, 0)
    back, ahead = hop_x(wide, 1), hop_x(wide, -1)
    near = join([after(p, back, ahead, a4), a1, b1, a2, b2])
    near_other = swap(near)
    a2, b2 = after(a2, back, ahead, a4), after(b2, back, ahead, a4)
    a3, b3 = hop(a2, 1, 0), hop(b2, -1, 0)
    across = hop_x(back, 1)

    panels = stack([wide, ahead, back], (0, 1, 3))
    near_steps, far_steps = (0, -1, 1, -2, 2), (-3, 3, -4)
    held = (0, 1, 3)
    (total,) = product(panels, [near, near_other], [(0, held, near_steps), (1, held, near_steps)])
    far = join([after(a3, across, total), b3, a4])
    far_other = swap(far)
    panels = stack([across], (2,), panels)
    every = (0, 1, 2, 3)
    rest = functools.partial(
        product,
        panels,
        [near, near_other, far, far_other],
        [(0, (2,), near_steps), (1, (2,), near_steps), (0, every, far_steps), (1, every, far_steps)],
        total,
    )

    (code,) = rest(slots=(3,), outs=(True,))
    passed = hop(code, 0, 1)
    code, side = rest(slots=(1, 2), outs=(True, False))
    sums = [hop(code, 0, -1)]
    code = call(
        relay_kernel,
        struct((ROWS + HEAD, TILE), jnp.int16),
        side,
        passed,
        scratch_shapes=[pltpu.VMEM((ROWS, TILE), jnp.float32)],
    )
    sums.append(hop(code, 0, 1))
    (own,) = rest(slots=(0,))
    keep, send, column = call(
        functools.partial(square_kernel, n_total / 32),
        [struct((half, TILE), jnp.float32)] * 2 + [struct((1, TILE), jnp.float32)],
        own,
        *sums,
    )
    column = jnp.concatenate([column, swap(column)])
    recv = swap(send)
    columns = [column] + [hop_x(column, d) for d in (1, -1, 2)]
    return call(
        functools.partial(scale_kernel, n_total),
        struct((half, 2 * TILE), jnp.float32),
        keep,
        recv,
        *columns,
    )


def solution(mesh):
    return jax.shard_map(
        on_device,
        mesh=mesh,
        in_specs=(
            P("row", ("col", "layer")),
            P(("col", "row"), "layer"),
            P("row", ("col", "layer")),
        ),
        out_specs=P(("row", "col"), "layer"),
        check_vma=False,
    )
```

```python
import functools

import jax
import jax.numpy as jnp
from jax import lax
from jax.experimental import pallas as pl
from jax.experimental.pallas import tpu as pltpu
from jax.sharding import PartitionSpec as P

TILE = 128
CAP = 8
HEAD = 16
SLAB = CAP * TILE + HEAD
NX, NY, NZ = 4, 4, 8
ROWS = 2048
LEVELS = 65535
FINE = 64
BATCH = 4
PIECES = 4
MIB = 1024 * 1024
VMEM = pl.BlockSpec(memory_space=pltpu.VMEM)
SMEM = pl.BlockSpec(memory_space=pltpu.SMEM)


def struct(shape, dtype):
    return jax.ShapeDtypeStruct(shape, dtype)


def call(kernel, out_shape, *operands, first=VMEM, mib=8, **kwargs):
    many = isinstance(out_shape, (list, tuple))
    return pl.pallas_call(
        kernel,
        out_shape=out_shape,
        in_specs=[first] + [VMEM] * (len(operands) - 1),
        out_specs=[VMEM] * len(out_shape) if many else VMEM,
        compiler_params=pltpu.CompilerParams(vmem_limit_bytes=mib * MIB),
        **kwargs,
    )(*operands)


def after(x, *others):
    return lax.optimization_barrier((x, *others))[0]


def hop(x, dz, dy):
    pairs = []
    for c in range(2):
        s = 1 - 2 * c
        for z in range(NZ):
            for y in range(NY):
                to = (z + s * dz) % NZ * NY + (y + s * dy) % NY
                pairs.append((c * NZ * NY + z * NY + y, c * NZ * NY + to))
    return lax.ppermute(x, ("col", "layer"), pairs)


def hop_x(x, dx):
    pairs = []
    for c in range(2):
        s = 1 - 2 * c
        pairs += [(i * 2 + c, (i + s * dx) % NX * 2 + c) for i in range(NX)]
    return lax.ppermute(x, ("row", "col"), pairs)


def swap(x):
    return lax.ppermute(x, "col", [(0, 1), (1, 0)])


def place():
    layer, core = lax.axis_index("layer"), lax.axis_index("col")
    return layer // NY, layer % NY, core, 1 - 2 * core


def pack_kernel(map_ref, a_ref, out_ref):
    lane = lax.broadcasted_iota(jnp.int32, (HEAD, TILE), 1)

    def step(t, carry):
        n, head = carry
        present = map_ref[0, t] != 0

        @pl.when(jnp.logical_and(present, n < CAP))
        def _():
            rows = pl.ds(pl.multiple_of(t * TILE, TILE), TILE)
            out_ref[pl.ds(pl.multiple_of(n * TILE, TILE), TILE), :] = a_ref[rows, :]

        head = jnp.where(jnp.logical_and(lane == n, present), t.astype(jnp.float32), head)
        return n + present.astype(jnp.int32), head

    count, head = lax.fori_loop(
        0, 16, step, (jnp.int32(0), jnp.zeros((HEAD, TILE), jnp.float32))
    )
    head = jnp.where(lane == CAP, count.astype(jnp.float32), head)
    out_ref[CAP * TILE :, :] = head.astype(out_ref.dtype)


def split_kernel(b_ref, keep_ref, send_ref):
    core = lax.axis_index("col")
    left, right = b_ref[:, :TILE], b_ref[:, TILE:]
    keep_ref[...] = jnp.where(core == 0, left, right)
    send_ref[...] = jnp.where(core == 0, right, left)


def block_kernel(keep_ref, recv_ref, *out_refs):
    _, y, _, s = place()
    for d, out_ref in zip((0, 1, -1, 2), out_refs):
        to = (y + s * d + NY) % NY
        for r, ref in enumerate((keep_ref, recv_ref)):
            for low in range(2):
                rows = pl.ds(pl.multiple_of((low * NY + to) * TILE, TILE), TILE)
                at = (r * 2 + low) * TILE
                out_ref[at : at + TILE, :] = ref[rows, :]


def widen_kernel(*refs):
    for i, ref in enumerate(refs[:-1]):
        refs[-1][:, i * TILE : (i + 1) * TILE] = ref[...]


def stack_kernel(places, *refs):
    out_ref = refs[-1]
    for place, ref in zip(places, refs):
        out_ref[place] = ref[...]


def stack(panels, places, whole=None):
    out = struct((NX, *panels[0].shape), panels[0].dtype)
    operands = panels + ([] if whole is None else [whole])
    alias = {} if whole is None else {len(panels): 0}
    return call(functools.partial(stack_kernel, places), out, *operands, input_output_aliases=alias)


def join_kernel(*refs):
    for i, ref in enumerate(refs[:-1]):
        refs[-1][i] = ref[...]


def join(parts):
    return call(join_kernel, struct((len(parts), *parts[0].shape), parts[0].dtype), *parts)


def product_kernel(plan, slots, outs, *refs):
    n = len(plan)
    b_ref, parts, given = refs[0], refs[1 : n + 1], refs[n + 1 : -5 - len(outs)]
    out_refs = refs[-5 - len(outs) : -5]
    total_ref, heads_ref, table_ref, work_ref, sem = refs[-5:]
    at = 0
    for part, (_, _, steps) in zip(parts, plan):
        for j in range(len(steps)):
            head = part[j, CAP * TILE :, :].astype(jnp.float32)
            heads_ref[at : at + 1, :] = head[0:1, :].astype(jnp.int32)
            at += 1
    copy = pltpu.make_async_copy(heads_ref, table_ref, sem)
    copy.start()
    lanes = slice(slots[0] * TILE, (slots[-1] + 1) * TILE)
    if given:
        total_ref[...] = given[0][:, lanes]
    else:
        total_ref[...] = jnp.zeros_like(total_ref)
    z, _, _, s = place()
    x = lax.axis_index("row")
    copy.wait()

    at = 0
    for part, (other, panels, steps) in zip(parts, plan):
        count = jnp.int32(0)
        for j, dz in enumerate(steps):
            source = (z + (-s if other else s) * dz + NZ) % NZ
            panel = ((source // 2 - x) * s + NX) % NX
            tiles = table_ref[at, CAP]
            if len(panels) < NX:
                held = functools.reduce(jnp.logical_or, [panel == k for k in panels])
                tiles = jnp.where(held, tiles, 0)

            def list_tile(i, count, j=j, at=at, source=source, other=other, panel=panel):
                work_ref[0, count] = j
                work_ref[1, count] = i
                work_ref[2, count] = table_ref[at, i]
                work_ref[3, count] = panel
                work_ref[4, count] = other * 2 + source % 2
                return count + 1

            count = lax.fori_loop(0, tiles, list_tile, count)
            at += 1
        for u in range(BATCH - 1):
            for k, v in enumerate((0, 0, ROWS // TILE, panels[0], 0)):
                work_ref[k, count + u] = v

        def step(g, carry, part=part):
            for u in range(BATCH):
                j, i, t, panel, at_b = (work_ref[k, g * BATCH + u] for k in range(5))
                rows = pl.ds(pl.multiple_of(t * TILE, TILE), TILE)
                total_ref[rows, :] += jnp.dot(
                    part[j, pl.ds(pl.multiple_of(i * TILE, TILE), TILE), :],
                    b_ref[panel, pl.ds(pl.multiple_of(at_b * TILE, TILE), TILE), lanes],
                    preferred_element_type=jnp.float32,
                )
            return carry

        lax.fori_loop(0, (count + BATCH - 1) // BATCH, step, 0)
    for i, (coded, out_ref) in enumerate(zip(outs, out_refs)):
        part = slice(i * TILE, (i + 1) * TILE)
        if coded:
            encode(total_ref, part, out_ref)
        elif len(outs) == 1:
            out_ref[...] = total_ref[...]
        else:
            out_ref[...] = total_ref[:, part]


def product(b_panels, parts, plan, total=None, slots=(0, 1, 2, 3), outs=(False,)):
    cols = len(slots) * TILE
    count = sum(len(steps) for _, _, steps in plan)
    flops = sum(p.size for p in parts) * cols * 2
    width = cols // len(outs)
    return call(
        functools.partial(product_kernel, tuple(plan), slots, outs),
        [
            struct((ROWS + HEAD, TILE), jnp.int16)
            if coded
            else struct((ROWS + TILE, width), jnp.float32)
            for coded in outs
        ],
        b_panels,
        *parts,
        *([] if total is None else [total]),
        mib=24,
        scratch_shapes=[
            pltpu.VMEM((ROWS + TILE, cols), jnp.float32),
            pltpu.VMEM((count, TILE), jnp.int32),
            pltpu.SMEM((count, TILE), jnp.int32),
            pltpu.SMEM((8, TILE), jnp.int32),
            pltpu.SemaphoreType.DMA(()),
        ],
        cost_estimate=pl.CostEstimate(flops=flops, bytes_accessed=flops // 128, transcendentals=0),
    )


def encode(total_ref, lanes, out_ref):
    top = total_ref[:TILE, lanes]
    for i in range(1, ROWS // TILE):
        top = jnp.maximum(top, total_ref[i * TILE : (i + 1) * TILE, lanes])
    top = jnp.maximum(jnp.max(top, axis=0, keepdims=True), jnp.float32(2.0**-100))
    exponent = jnp.ceil(jnp.log2(top) * FINE)
    inverse = LEVELS * jnp.exp2(exponent * (-1.0 / FINE))
    for i in range(ROWS // TILE):
        part = slice(i * TILE, (i + 1) * TILE)
        steps = jnp.minimum(total_ref[part, lanes] * inverse + 0.5, jnp.float32(LEVELS))
        out_ref[part, :] = (steps.astype(jnp.int32) - 32768).astype(jnp.int16)
    exponent = jnp.broadcast_to(exponent, (HEAD, TILE)).astype(jnp.int32)
    out_ref[ROWS:, :] = exponent.astype(jnp.int16)


def scale_of(ref):
    exponent = ref[ROWS:, :].astype(jnp.int32).astype(jnp.float32)[0:1, :]
    return jnp.exp2(exponent * (1.0 / FINE)) * jnp.float32(1.0 / LEVELS)


def decode(ref, part, scale):
    return (ref[part, :].astype(jnp.int32) + 32768).astype(jnp.float32) * scale


def relay_kernel(total_ref, recv_ref, out_ref, sum_ref):
    scale = scale_of(recv_ref)
    for i in range(ROWS // TILE):
        part = slice(i * TILE, (i + 1) * TILE)
        sum_ref[part, :] = total_ref[part, :] + decode(recv_ref, part, scale)
    encode(sum_ref, slice(0, TILE), out_ref)


def square_kernel(weight, total_ref, *refs):
    recv, (keep_ref, send_ref, sum_ref) = refs[:2], refs[2:]
    core = lax.axis_index("col")
    first_col = lax.axis_index("layer") * 2 * TILE + core * TILE
    scales = [scale_of(ref) for ref in recv]
    row = lax.broadcasted_iota(jnp.int32, (TILE, TILE), 0)
    col = lax.broadcasted_iota(jnp.int32, (TILE, TILE), 1)
    column = jnp.zeros((TILE, TILE), jnp.float32)
    half = ROWS // 2
    for i in range(half // TILE):
        for own, out_ref in ((1, keep_ref), (0, send_ref)):
            start = (core if own else 1 - core) * half + i * TILE
            part = pl.ds(pl.multiple_of(start, TILE), TILE)
            first_row = lax.axis_index("row") * ROWS + start
            diagonal = row + (first_row - first_col) == col
            expanded = total_ref[part, :] + jnp.where(
                diagonal, jnp.float32(weight), jnp.float32(0)
            )
            for ref, scale in zip(recv, scales):
                expanded += decode(ref, part, scale)
            power = expanded * expanded
            out_ref[i * TILE : (i + 1) * TILE, :] = power
            column += power
    sum_ref[...] = jnp.sum(column, axis=0, keepdims=True)


def scale_kernel(n_total, keep_ref, recv_ref, *refs):
    sums, (out_hbm, out_ref, sems) = refs[:-3], refs[-3:]
    total = sums[0][...]
    for ref in sums[1:]:
        total += ref[...]
    core = lax.axis_index("col")
    rows = keep_ref.shape[0] // PIECES
    copies = []
    for i in range(PIECES):
        part = slice(i * rows, (i + 1) * rows)
        own = jnp.float32(n_total) * keep_ref[part, :] / total[0:1, :]
        other = jnp.float32(n_total) * recv_ref[part, :] / total[1:2, :]
        out_ref[part, :TILE] = jnp.where(core == 0, own, other)
        out_ref[part, TILE:] = jnp.where(core == 0, other, own)
        copies.append(
            pltpu.make_async_copy(out_ref.at[part, :], out_hbm.at[part, :], sems.at[i])
        )
        copies[-1].start()
    for copy in copies:
        copy.wait()


def scale(n_total, keep, recv, sums):
    shape = (keep.shape[0], 2 * TILE)
    return pl.pallas_call(
        functools.partial(scale_kernel, n_total),
        out_shape=struct(shape, jnp.float32),
        in_specs=[VMEM] * (2 + len(sums)),
        out_specs=pl.BlockSpec(memory_space=pl.ANY),
        scratch_shapes=[pltpu.VMEM(shape, jnp.float32), pltpu.SemaphoreType.DMA((PIECES,))],
        compiler_params=pltpu.CompilerParams(vmem_limit_bytes=8 * MIB),
    )(keep, recv, *sums)


def on_device(a_matrix, b_matrix, tile_map):
    n_total = a_matrix.shape[1] * 64
    half = ROWS // 2
    keep, send = call(split_kernel, [struct((half, TILE), b_matrix.dtype)] * 2, b_matrix)
    recv = swap(send)
    p = call(
        pack_kernel,
        struct((SLAB, TILE), a_matrix.dtype),
        tile_map.reshape(1, 16),
        a_matrix,
        first=SMEM,
    )
    a1, b1 = hop(p, 1, 0), hop(p, -1, 0)
    blocks = call(block_kernel, [struct((512, TILE), b_matrix.dtype)] * 4, after(keep, p), recv)
    far_y = hop(blocks[3], 0, 2)
    blocks = [blocks[0], hop(blocks[1], 0, 1), hop(blocks[2], 0, -1), far_y]
    wide = call(widen_kernel, struct((512, 4 * TILE), b_matrix.dtype), *blocks)

    a1, b1 = after(a1, wide), after(b1, wide)
    a3, a2, b2 = hop(a1, 2, 0), hop(a1, 1, 0), hop(b1, -1, 0)
    back, ahead = hop_x(wide, 1), hop_x(wide, -1)
    near = join([after(p, back, ahead), a1, b1, a2, b2, a3])
    near_other = swap(near)
    a4, b3 = hop(after(a3, back, ahead), 1, 0), hop(after(b2, back, ahead), -1, 0)
    across = hop_x(back, 1)

    panels = stack([wide, ahead, back], (0, 1, 3))
    near_steps, far_steps = (0, -1, 1, -2, 2, -3), (3, -4)
    held = (0, 1, 3)
    (total,) = product(panels, [near, near_other], [(0, held, near_steps), (1, held, near_steps)])
    far = join([after(b3, across, total), a4])
    far_other = swap(far)
    panels = stack([across], (2,), panels)
    every = (0, 1, 2, 3)
    rest = functools.partial(
        product,
        panels,
        [near, near_other, far, far_other],
        [(0, (2,), near_steps), (1, (2,), near_steps), (0, every, far_steps), (1, every, far_steps)],
        total,
    )

    (code,) = rest(slots=(3,), outs=(True,))
    passed = hop(code, 0, 1)
    code, side = rest(slots=(1, 2), outs=(True, False))
    sums = [hop(code, 0, -1)]
    code = call(
        relay_kernel,
        struct((ROWS + HEAD, TILE), jnp.int16),
        side,
        passed,
        scratch_shapes=[pltpu.VMEM((ROWS, TILE), jnp.float32)],
    )
    sums.append(hop(code, 0, 1))
    (own,) = rest(slots=(0,))
    keep, send, column = call(
        functools.partial(square_kernel, n_total / 32),
        [struct((half, TILE), jnp.float32)] * 2 + [struct((1, TILE), jnp.float32)],
        own,
        *sums,
    )
    column = jnp.concatenate([column, swap(column)])
    recv = swap(after(send, column))
    columns = [column] + [hop_x(column, d) for d in (1, -1, 2)]
    return scale(n_total, keep, recv, columns)


def solution(mesh):
    return jax.shard_map(
        on_device,
        mesh=mesh,
        in_specs=(
            P("row", ("col", "layer")),
            P(("col", "row"), "layer"),
            P("row", ("col", "layer")),
        ),
        out_specs=P(("row", "col"), "layer"),
        check_vma=False,
    )
```

```python
import functools

import jax
import jax.numpy as jnp
from jax import lax
from jax.experimental import pallas as pl
from jax.experimental.pallas import tpu as pltpu
from jax.sharding import PartitionSpec as P

TILE = 128
CAP = 8
HEAD = 16
SLAB = CAP * TILE + HEAD
NX, NY, NZ = 4, 4, 8
ROWS = 2048
LEVELS = 65535
FINE = 64
BATCH = 8
PIECES = 4
MIB = 1024 * 1024
VMEM = pl.BlockSpec(memory_space=pltpu.VMEM)
SMEM = pl.BlockSpec(memory_space=pltpu.SMEM)


def struct(shape, dtype):
    return jax.ShapeDtypeStruct(shape, dtype)


def call(kernel, out_shape, *operands, first=VMEM, mib=8, **kwargs):
    many = isinstance(out_shape, (list, tuple))
    return pl.pallas_call(
        kernel,
        out_shape=out_shape,
        in_specs=[first] + [VMEM] * (len(operands) - 1),
        out_specs=[VMEM] * len(out_shape) if many else VMEM,
        compiler_params=pltpu.CompilerParams(vmem_limit_bytes=mib * MIB),
        **kwargs,
    )(*operands)


def after(x, *others):
    return lax.optimization_barrier((x, *others))[0]


def hop(x, dz, dy):
    pairs = []
    for c in range(2):
        s = 1 - 2 * c
        for z in range(NZ):
            for y in range(NY):
                to = (z + s * dz) % NZ * NY + (y + s * dy) % NY
                pairs.append((c * NZ * NY + z * NY + y, c * NZ * NY + to))
    return lax.ppermute(x, ("col", "layer"), pairs)


def hop_x(x, dx):
    pairs = []
    for c in range(2):
        s = 1 - 2 * c
        pairs += [(i * 2 + c, (i + s * dx) % NX * 2 + c) for i in range(NX)]
    return lax.ppermute(x, ("row", "col"), pairs)


def swap(x):
    return lax.ppermute(x, "col", [(0, 1), (1, 0)])


def place():
    layer, core = lax.axis_index("layer"), lax.axis_index("col")
    return layer // NY, layer % NY, core, 1 - 2 * core


def pack_kernel(map_ref, a_ref, out_ref):
    lane = lax.broadcasted_iota(jnp.int32, (HEAD, TILE), 1)

    def step(t, carry):
        n, head = carry
        present = map_ref[0, t] != 0

        @pl.when(jnp.logical_and(present, n < CAP))
        def _():
            rows = pl.ds(pl.multiple_of(t * TILE, TILE), TILE)
            out_ref[pl.ds(pl.multiple_of(n * TILE, TILE), TILE), :] = a_ref[rows, :]

        head = jnp.where(jnp.logical_and(lane == n, present), t.astype(jnp.float32), head)
        return n + present.astype(jnp.int32), head

    count, head = lax.fori_loop(
        0, 16, step, (jnp.int32(0), jnp.zeros((HEAD, TILE), jnp.float32))
    )
    head = jnp.where(lane == CAP, count.astype(jnp.float32), head)
    out_ref[CAP * TILE :, :] = head.astype(out_ref.dtype)


def split_kernel(b_ref, keep_ref, send_ref):
    core = lax.axis_index("col")
    left, right = b_ref[:, :TILE], b_ref[:, TILE:]
    keep_ref[...] = jnp.where(core == 0, left, right)
    send_ref[...] = jnp.where(core == 0, right, left)


def block_kernel(keep_ref, recv_ref, *out_refs):
    _, y, _, s = place()
    for d, out_ref in zip((0, 1, -1, 2), out_refs):
        to = (y + s * d + NY) % NY
        for r, ref in enumerate((keep_ref, recv_ref)):
            for low in range(2):
                rows = pl.ds(pl.multiple_of((low * NY + to) * TILE, TILE), TILE)
                at = (r * 2 + low) * TILE
                out_ref[at : at + TILE, :] = ref[rows, :]


def widen_kernel(*refs):
    for i, ref in enumerate(refs[:-1]):
        refs[-1][:, i * TILE : (i + 1) * TILE] = ref[...]


def stack_kernel(places, *refs):
    out_ref = refs[-1]
    for place, ref in zip(places, refs):
        out_ref[place] = ref[...]


def stack(panels, places, whole=None):
    out = struct((NX, *panels[0].shape), panels[0].dtype)
    operands = panels + ([] if whole is None else [whole])
    alias = {} if whole is None else {len(panels): 0}
    return call(functools.partial(stack_kernel, places), out, *operands, input_output_aliases=alias)


def join_kernel(*refs):
    for i, ref in enumerate(refs[:-1]):
        refs[-1][i] = ref[...]


def join(parts):
    return call(join_kernel, struct((len(parts), *parts[0].shape), parts[0].dtype), *parts)


def product_kernel(plan, slots, outs, *refs):
    n = len(plan)
    b_ref, parts, given = refs[0], refs[1 : n + 1], refs[n + 1 : -5 - len(outs)]
    out_refs = refs[-5 - len(outs) : -5]
    total_ref, heads_ref, table_ref, work_ref, sem = refs[-5:]
    at = 0
    for part, (_, _, steps) in zip(parts, plan):
        for j in range(len(steps)):
            head = part[j, CAP * TILE :, :].astype(jnp.float32)
            heads_ref[at : at + 1, :] = head[0:1, :].astype(jnp.int32)
            at += 1
    copy = pltpu.make_async_copy(heads_ref, table_ref, sem)
    copy.start()
    lanes = slice(slots[0] * TILE, (slots[-1] + 1) * TILE)
    if given:
        total_ref[...] = given[0][:, lanes]
    else:
        total_ref[...] = jnp.zeros_like(total_ref)
    z, _, _, s = place()
    x = lax.axis_index("row")
    copy.wait()

    at = 0
    for part, (other, panels, steps) in zip(parts, plan):
        count = jnp.int32(0)
        for j, dz in enumerate(steps):
            source = (z + (-s if other else s) * dz + NZ) % NZ
            panel = ((source // 2 - x) * s + NX) % NX
            tiles = table_ref[at, CAP]
            if len(panels) < NX:
                held = functools.reduce(jnp.logical_or, [panel == k for k in panels])
                tiles = jnp.where(held, tiles, 0)

            def list_tile(i, count, j=j, at=at, source=source, other=other, panel=panel):
                work_ref[0, count] = j
                work_ref[1, count] = i
                work_ref[2, count] = table_ref[at, i]
                work_ref[3, count] = panel
                work_ref[4, count] = other * 2 + source % 2
                return count + 1

            count = lax.fori_loop(0, tiles, list_tile, count)
            at += 1
        for u in range(BATCH - 1):
            for k, v in enumerate((0, 0, ROWS // TILE, panels[0], 0)):
                work_ref[k, count + u] = v

        def step(g, carry, part=part):
            for u in range(BATCH):
                j, i, t, panel, at_b = (work_ref[k, g * BATCH + u] for k in range(5))
                rows = pl.ds(pl.multiple_of(t * TILE, TILE), TILE)
                total_ref[rows, :] += jnp.dot(
                    part[j, pl.ds(pl.multiple_of(i * TILE, TILE), TILE), :],
                    b_ref[panel, pl.ds(pl.multiple_of(at_b * TILE, TILE), TILE), lanes],
                    preferred_element_type=jnp.float32,
                )
            return carry

        lax.fori_loop(0, (count + BATCH - 1) // BATCH, step, 0)
    for out, out_ref in zip(outs, out_refs):
        if out is None:
            out_ref[...] = total_ref[...]
        elif isinstance(out, int):
            out_ref[...] = total_ref[:, out * TILE : (out + 1) * TILE]
        else:
            slot, start, _ = out
            encode(total_ref, slice(slot * TILE, (slot + 1) * TILE), out_ref, start)


def product(b_panels, parts, plan, total=None, slots=(0, 1, 2, 3), outs=(None,)):
    cols = len(slots) * TILE
    count = sum(len(steps) for _, _, steps in plan)
    flops = sum(p.size for p in parts) * cols * 2
    return call(
        functools.partial(product_kernel, tuple(plan), slots, outs),
        [
            struct((out[2] + HEAD, TILE), jnp.int16)
            if isinstance(out, tuple)
            else struct((ROWS + TILE, cols if out is None else TILE), jnp.float32)
            for out in outs
        ],
        b_panels,
        *parts,
        *([] if total is None else [total]),
        mib=24,
        scratch_shapes=[
            pltpu.VMEM((ROWS + TILE, cols), jnp.float32),
            pltpu.VMEM((count, TILE), jnp.int32),
            pltpu.SMEM((count, TILE), jnp.int32),
            pltpu.SMEM((8, TILE), jnp.int32),
            pltpu.SemaphoreType.DMA(()),
        ],
        cost_estimate=pl.CostEstimate(flops=flops, bytes_accessed=flops // 128, transcendentals=0),
    )


def encode(total_ref, lanes, out_ref, start):
    rows = out_ref.shape[0] - HEAD
    top = total_ref[start : start + TILE, lanes]
    for i in range(TILE, rows, TILE):
        top = jnp.maximum(top, total_ref[start + i : start + i + TILE, lanes])
    top = jnp.maximum(jnp.max(top, axis=0, keepdims=True), jnp.float32(2.0**-100))
    exponent = jnp.ceil(jnp.log2(top) * FINE)
    inverse = LEVELS * jnp.exp2(exponent * (-1.0 / FINE))
    for i in range(0, rows, TILE):
        sums = total_ref[start + i : start + i + TILE, lanes]
        steps = jnp.minimum(sums * inverse + 0.5, jnp.float32(LEVELS))
        out_ref[i : i + TILE, :] = (steps.astype(jnp.int32) - 32768).astype(jnp.int16)
    exponent = jnp.broadcast_to(exponent, (HEAD, TILE)).astype(jnp.int32)
    out_ref[rows:, :] = exponent.astype(jnp.int16)


def scale_of(ref):
    exponent = ref[ref.shape[0] - HEAD :, :].astype(jnp.int32).astype(jnp.float32)[0:1, :]
    return jnp.exp2(exponent * (1.0 / FINE)) * jnp.float32(1.0 / LEVELS)


def decode(ref, start, scale):
    steps = ref[start : start + TILE, :].astype(jnp.int32) + 32768
    return steps.astype(jnp.float32) * scale


def relay_kernel(start, total_ref, recv_ref, out_ref, sum_ref):
    scale = scale_of(recv_ref)
    for i in range(0, ROWS // 2, TILE):
        sum_ref[i : i + TILE, :] = total_ref[start + i : start + i + TILE, :] + decode(
            recv_ref, i, scale
        )
    encode(sum_ref, slice(0, TILE), out_ref, 0)


def relay(side, passed, start):
    return call(
        functools.partial(relay_kernel, start),
        struct(passed.shape, jnp.int16),
        side,
        passed,
        scratch_shapes=[pltpu.VMEM((ROWS // 2, TILE), jnp.float32)],
    )


def square_kernel(weight, total_ref, whole_ref, low_ref, high_ref, keep_ref, send_ref, sum_ref):
    core = lax.axis_index("col")
    first_col = lax.axis_index("layer") * 2 * TILE + core * TILE
    whole_scale, scales = scale_of(whole_ref), [scale_of(ref) for ref in (low_ref, high_ref)]
    row = lax.broadcasted_iota(jnp.int32, (TILE, TILE), 0)
    col = lax.broadcasted_iota(jnp.int32, (TILE, TILE), 1)
    column = jnp.zeros((TILE, TILE), jnp.float32)
    half = ROWS // 2
    for i in range(0, half, TILE):
        powers = []
        for start, ref, scale in ((0, low_ref, scales[0]), (half, high_ref, scales[1])):
            first_row = lax.axis_index("row") * ROWS + start + i
            diagonal = row + (first_row - first_col) == col
            expanded = total_ref[start + i : start + i + TILE, :] + jnp.where(
                diagonal, jnp.float32(weight), jnp.float32(0)
            )
            expanded += decode(whole_ref, start + i, whole_scale) + decode(ref, i, scale)
            powers.append(expanded * expanded)
            column += powers[-1]
        keep_ref[i : i + TILE, :] = jnp.where(core == 0, powers[0], powers[1])
        send_ref[i : i + TILE, :] = jnp.where(core == 0, powers[1], powers[0])
    sum_ref[...] = jnp.sum(column, axis=0, keepdims=True)


def scale_kernel(n_total, keep_ref, recv_ref, *refs):
    sums, (out_hbm, out_ref, sems) = refs[:-3], refs[-3:]
    total = sums[0][...]
    for ref in sums[1:]:
        total += ref[...]
    core = lax.axis_index("col")
    rows = keep_ref.shape[0] // PIECES
    copies = []
    for i in range(PIECES):
        part = slice(i * rows, (i + 1) * rows)
        own = jnp.float32(n_total) * keep_ref[part, :] / total[0:1, :]
        other = jnp.float32(n_total) * recv_ref[part, :] / total[1:2, :]
        out_ref[part, :TILE] = jnp.where(core == 0, own, other)
        out_ref[part, TILE:] = jnp.where(core == 0, other, own)
        copies.append(
            pltpu.make_async_copy(out_ref.at[part, :], out_hbm.at[part, :], sems.at[i])
        )
        copies[-1].start()
    for copy in copies:
        copy.wait()


def scale(n_total, keep, recv, sums):
    shape = (keep.shape[0], 2 * TILE)
    return pl.pallas_call(
        functools.partial(scale_kernel, n_total),
        out_shape=struct(shape, jnp.float32),
        in_specs=[VMEM] * (2 + len(sums)),
        out_specs=pl.BlockSpec(memory_space=pl.ANY),
        scratch_shapes=[pltpu.VMEM(shape, jnp.float32), pltpu.SemaphoreType.DMA((PIECES,))],
        compiler_params=pltpu.CompilerParams(vmem_limit_bytes=8 * MIB),
    )(keep, recv, *sums)


def on_device(a_matrix, b_matrix, tile_map):
    n_total = a_matrix.shape[1] * 64
    half = ROWS // 2
    keep, send = call(split_kernel, [struct((half, TILE), b_matrix.dtype)] * 2, b_matrix)
    recv = swap(send)
    p = call(
        pack_kernel,
        struct((SLAB, TILE), a_matrix.dtype),
        tile_map.reshape(1, 16),
        a_matrix,
        first=SMEM,
    )
    a1, b1 = hop(p, 1, 0), hop(p, -1, 0)
    blocks = call(block_kernel, [struct((512, TILE), b_matrix.dtype)] * 4, after(keep, p), recv)
    far_y = hop(blocks[3], 0, 2)
    blocks = [blocks[0], hop(blocks[1], 0, 1), hop(blocks[2], 0, -1), far_y]
    wide = call(widen_kernel, struct((512, 4 * TILE), b_matrix.dtype), *blocks)

    a1, b1 = after(a1, wide), after(b1, wide)
    a3, a2, b2 = hop(a1, 2, 0), hop(a1, 1, 0), hop(b1, -1, 0)
    back, ahead = hop_x(wide, 1), hop_x(wide, -1)
    near = join([after(p, back, ahead), a1, b1, a2, b2, a3])
    near_other = swap(near)
    a4, b3 = hop(after(a3, back, ahead), 1, 0), hop(after(b2, back, ahead), -1, 0)
    across = hop_x(back, 1)

    panels = stack([wide, ahead, back], (0, 1, 3))
    near_steps, far_steps = (0, -1, 1, -2, 2, -3), (3, -4)
    held = (0, 1, 3)
    (total,) = product(panels, [near, near_other], [(0, held, near_steps), (1, held, near_steps)])
    far = join([after(b3, across, total), a4])
    far_other = swap(far)
    panels = stack([across], (2,), panels)
    every = (0, 1, 2, 3)
    rest = functools.partial(
        product,
        panels,
        [near, near_other, far, far_other],
        [(0, (2,), near_steps), (1, (2,), near_steps), (0, every, far_steps), (1, every, far_steps)],
        total,
    )

    low, high = rest(slots=(3,), outs=((0, 0, half), (0, half, half)))
    low, high = hop(low, 0, 1), hop(high, 0, 1)
    code, side = rest(slots=(1, 2), outs=((0, 0, ROWS), 1))
    sums = [hop(code, 0, -1)]
    sums.append(hop(relay(side, low, 0), 0, 1))
    sums.append(hop(relay(side, high, half), 0, 1))
    (own,) = rest(slots=(0,))
    keep, send, column = call(
        functools.partial(square_kernel, n_total / 32),
        [struct((half, TILE), jnp.float32)] * 2 + [struct((1, TILE), jnp.float32)],
        own,
        *sums,
    )
    column = jnp.concatenate([column, swap(column)])
    recv = swap(after(send, column))
    columns = [column] + [hop_x(column, d) for d in (1, -1, 2)]
    return scale(n_total, keep, recv, columns)


def solution(mesh):
    return jax.shard_map(
        on_device,
        mesh=mesh,
        in_specs=(
            P("row", ("col", "layer")),
            P(("col", "row"), "layer"),
            P("row", ("col", "layer")),
        ),
        out_specs=P(("row", "col"), "layer"),
        check_vma=False,
    )
```

```python
import functools

import jax
import jax.numpy as jnp
from jax import lax
from jax.experimental import pallas as pl
from jax.experimental.pallas import tpu as pltpu
from jax.sharding import PartitionSpec as P

TILE = 128
CAP = 8
HEAD = 16
SLAB = CAP * TILE + HEAD
NX, NY, NZ = 4, 4, 8
ROWS = 2048
LEVELS = 65535
FINE = 64
BATCH = 8
PIECES = 4
MIB = 1024 * 1024
VMEM = pl.BlockSpec(memory_space=pltpu.VMEM)
SMEM = pl.BlockSpec(memory_space=pltpu.SMEM)


def struct(shape, dtype):
    return jax.ShapeDtypeStruct(shape, dtype)


def call(kernel, out_shape, *operands, first=VMEM, mib=8, **kwargs):
    many = isinstance(out_shape, (list, tuple))
    return pl.pallas_call(
        kernel,
        out_shape=out_shape,
        in_specs=[first] + [VMEM] * (len(operands) - 1),
        out_specs=[VMEM] * len(out_shape) if many else VMEM,
        compiler_params=pltpu.CompilerParams(vmem_limit_bytes=mib * MIB),
        **kwargs,
    )(*operands)


def after(x, *others):
    return lax.optimization_barrier((x, *others))[0]


def hop(x, dz, dy):
    pairs = []
    for c in range(2):
        s = 1 - 2 * c
        for z in range(NZ):
            for y in range(NY):
                to = (z + s * dz) % NZ * NY + (y + s * dy) % NY
                pairs.append((c * NZ * NY + z * NY + y, c * NZ * NY + to))
    return lax.ppermute(x, ("col", "layer"), pairs)


def hop_x(x, dx):
    pairs = []
    for c in range(2):
        s = 1 - 2 * c
        pairs += [(i * 2 + c, (i + s * dx) % NX * 2 + c) for i in range(NX)]
    return lax.ppermute(x, ("row", "col"), pairs)


def swap(x):
    return lax.ppermute(x, "col", [(0, 1), (1, 0)])


def place():
    layer, core = lax.axis_index("layer"), lax.axis_index("col")
    return layer // NY, layer % NY, core, 1 - 2 * core


def pack_kernel(map_ref, a_ref, out_ref):
    lane = lax.broadcasted_iota(jnp.int32, (HEAD, TILE), 1)

    def step(t, carry):
        n, head = carry
        present = map_ref[0, t] != 0

        @pl.when(jnp.logical_and(present, n < CAP))
        def _():
            rows = pl.ds(pl.multiple_of(t * TILE, TILE), TILE)
            out_ref[pl.ds(pl.multiple_of(n * TILE, TILE), TILE), :] = a_ref[rows, :]

        head = jnp.where(jnp.logical_and(lane == n, present), t.astype(jnp.float32), head)
        return n + present.astype(jnp.int32), head

    count, head = lax.fori_loop(
        0, 16, step, (jnp.int32(0), jnp.zeros((HEAD, TILE), jnp.float32))
    )
    head = jnp.where(lane == CAP, count.astype(jnp.float32), head)
    out_ref[CAP * TILE :, :] = head.astype(out_ref.dtype)


def split_kernel(b_ref, keep_ref, send_ref):
    core = lax.axis_index("col")
    left, right = b_ref[:, :TILE], b_ref[:, TILE:]
    keep_ref[...] = jnp.where(core == 0, left, right)
    send_ref[...] = jnp.where(core == 0, right, left)


def block_kernel(keep_ref, recv_ref, *out_refs):
    _, y, _, s = place()
    for d, out_ref in zip((0, 1, -1, 2), out_refs):
        to = (y + s * d + NY) % NY
        for r, ref in enumerate((keep_ref, recv_ref)):
            for low in range(2):
                rows = pl.ds(pl.multiple_of((low * NY + to) * TILE, TILE), TILE)
                at = (r * 2 + low) * TILE
                out_ref[at : at + TILE, :] = ref[rows, :]


def widen_kernel(*refs):
    for i, ref in enumerate(refs[:-1]):
        refs[-1][:, i * TILE : (i + 1) * TILE] = ref[...]


def stack_kernel(places, *refs):
    out_ref = refs[-1]
    for place, ref in zip(places, refs):
        out_ref[place] = ref[...]


def stack(panels, places, whole=None):
    out = struct((NX, *panels[0].shape), panels[0].dtype)
    operands = panels + ([] if whole is None else [whole])
    alias = {} if whole is None else {len(panels): 0}
    return call(functools.partial(stack_kernel, places), out, *operands, input_output_aliases=alias)


def join_kernel(*refs):
    for i, ref in enumerate(refs[:-1]):
        refs[-1][i] = ref[...]


def join(parts):
    return call(join_kernel, struct((len(parts), *parts[0].shape), parts[0].dtype), *parts)


def product_kernel(plan, slots, outs, *refs):
    n = len(plan)
    b_ref, parts, given = refs[0], refs[1 : n + 1], refs[n + 1 : -5 - len(outs)]
    out_refs = refs[-5 - len(outs) : -5]
    total_ref, heads_ref, table_ref, work_ref, sem = refs[-5:]
    if outs == (None,):
        total_ref = out_refs[0]
    at = 0
    for part, (_, _, steps) in zip(parts, plan):
        for j in range(len(steps)):
            head = part[j, CAP * TILE :, :].astype(jnp.float32)
            heads_ref[at : at + 1, :] = head[0:1, :].astype(jnp.int32)
            at += 1
    copy = pltpu.make_async_copy(heads_ref, table_ref, sem)
    copy.start()
    lanes = slice(slots[0] * TILE, (slots[-1] + 1) * TILE)
    if given:
        total_ref[...] = given[0][:, lanes]
    else:
        total_ref[...] = jnp.zeros_like(total_ref)
    z, _, _, s = place()
    x = lax.axis_index("row")
    copy.wait()

    at = 0
    for part, (other, panels, steps) in zip(parts, plan):
        count = jnp.int32(0)
        for j, dz in enumerate(steps):
            source = (z + (-s if other else s) * dz + NZ) % NZ
            panel = ((source // 2 - x) * s + NX) % NX
            tiles = table_ref[at, CAP]
            if len(panels) < NX:
                held = functools.reduce(jnp.logical_or, [panel == k for k in panels])
                tiles = jnp.where(held, tiles, 0)

            def list_tile(i, count, j=j, at=at, source=source, other=other, panel=panel):
                work_ref[0, count] = j
                work_ref[1, count] = i
                work_ref[2, count] = table_ref[at, i]
                work_ref[3, count] = panel
                work_ref[4, count] = other * 2 + source % 2
                return count + 1

            count = lax.fori_loop(0, tiles, list_tile, count)
            at += 1
        for u in range(BATCH - 1):
            for k, v in enumerate((0, 0, ROWS // TILE, panels[0], 0)):
                work_ref[k, count + u] = v

        def step(g, carry, part=part):
            for u in range(BATCH):
                j, i, t, panel, at_b = (work_ref[k, g * BATCH + u] for k in range(5))
                rows = pl.ds(pl.multiple_of(t * TILE, TILE), TILE)
                total_ref[rows, :] += jnp.dot(
                    part[j, pl.ds(pl.multiple_of(i * TILE, TILE), TILE), :],
                    b_ref[panel, pl.ds(pl.multiple_of(at_b * TILE, TILE), TILE), lanes],
                    preferred_element_type=jnp.float32,
                )
            return carry

        lax.fori_loop(0, (count + BATCH - 1) // BATCH, step, 0)
    for out, out_ref in zip(outs, out_refs):
        if out is None:
            continue
        if isinstance(out, int):
            out_ref[...] = total_ref[:, out * TILE : (out + 1) * TILE]
        else:
            slot, start, _ = out
            encode(total_ref, slice(slot * TILE, (slot + 1) * TILE), out_ref, start)


def product(b_panels, parts, plan, total=None, slots=(0, 1, 2, 3), outs=(None,)):
    cols = len(slots) * TILE
    count = sum(len(steps) for _, _, steps in plan)
    flops = sum(p.size for p in parts) * cols * 2
    return call(
        functools.partial(product_kernel, tuple(plan), slots, outs),
        [
            struct((out[2] + HEAD, TILE), jnp.int16)
            if isinstance(out, tuple)
            else struct((ROWS + TILE, cols if out is None else TILE), jnp.float32)
            for out in outs
        ],
        b_panels,
        *parts,
        *([] if total is None else [total]),
        mib=24,
        scratch_shapes=[
            pltpu.VMEM((8 if outs == (None,) else ROWS + TILE, cols), jnp.float32),
            pltpu.VMEM((count, TILE), jnp.int32),
            pltpu.SMEM((count, TILE), jnp.int32),
            pltpu.SMEM((8, TILE), jnp.int32),
            pltpu.SemaphoreType.DMA(()),
        ],
        cost_estimate=pl.CostEstimate(flops=flops, bytes_accessed=flops // 128, transcendentals=0),
    )


def encode(total_ref, lanes, out_ref, start):
    rows = out_ref.shape[0] - HEAD
    top = total_ref[start : start + TILE, lanes]
    for i in range(TILE, rows, TILE):
        top = jnp.maximum(top, total_ref[start + i : start + i + TILE, lanes])
    top = jnp.maximum(jnp.max(top, axis=0, keepdims=True), jnp.float32(2.0**-100))
    exponent = jnp.ceil(jnp.log2(top) * FINE)
    inverse = LEVELS * jnp.exp2(exponent * (-1.0 / FINE))
    for i in range(0, rows, TILE):
        sums = total_ref[start + i : start + i + TILE, lanes]
        steps = jnp.minimum(sums * inverse + 0.5, jnp.float32(LEVELS))
        out_ref[i : i + TILE, :] = (steps.astype(jnp.int32) - 32768).astype(jnp.int16)
    exponent = jnp.broadcast_to(exponent, (HEAD, TILE)).astype(jnp.int32)
    out_ref[rows:, :] = exponent.astype(jnp.int16)


def scale_of(ref):
    exponent = ref[ref.shape[0] - HEAD :, :].astype(jnp.int32).astype(jnp.float32)[0:1, :]
    return jnp.exp2(exponent * (1.0 / FINE)) * jnp.float32(1.0 / LEVELS)


def decode(ref, start, scale):
    steps = ref[start : start + TILE, :].astype(jnp.int32) + 32768
    return steps.astype(jnp.float32) * scale


def relay_kernel(start, total_ref, recv_ref, out_ref, sum_ref):
    scale = scale_of(recv_ref)
    for i in range(0, ROWS // 2, TILE):
        sum_ref[i : i + TILE, :] = total_ref[start + i : start + i + TILE, :] + decode(
            recv_ref, i, scale
        )
    encode(sum_ref, slice(0, TILE), out_ref, 0)


def relay(side, passed, start):
    return call(
        functools.partial(relay_kernel, start),
        struct(passed.shape, jnp.int16),
        side,
        passed,
        scratch_shapes=[pltpu.VMEM((ROWS // 2, TILE), jnp.float32)],
    )


def square_kernel(weight, total_ref, whole_ref, low_ref, high_ref, keep_ref, send_ref, sum_ref):
    core = lax.axis_index("col")
    first_col = lax.axis_index("layer") * 2 * TILE + core * TILE
    whole_scale, scales = scale_of(whole_ref), [scale_of(ref) for ref in (low_ref, high_ref)]
    row = lax.broadcasted_iota(jnp.int32, (TILE, TILE), 0)
    col = lax.broadcasted_iota(jnp.int32, (TILE, TILE), 1)
    column = jnp.zeros((TILE, TILE), jnp.float32)
    half = ROWS // 2
    for i in range(0, half, TILE):
        powers = []
        for start, ref, scale in ((0, low_ref, scales[0]), (half, high_ref, scales[1])):
            first_row = lax.axis_index("row") * ROWS + start + i
            diagonal = row + (first_row - first_col) == col
            expanded = total_ref[start + i : start + i + TILE, :] + jnp.where(
                diagonal, jnp.float32(weight), jnp.float32(0)
            )
            expanded += decode(whole_ref, start + i, whole_scale) + decode(ref, i, scale)
            powers.append(expanded * expanded)
            column += powers[-1]
        keep_ref[i : i + TILE, :] = jnp.where(core == 0, powers[0], powers[1])
        send_ref[i : i + TILE, :] = jnp.where(core == 0, powers[1], powers[0])
    sum_ref[...] = jnp.sum(column, axis=0, keepdims=True)


def scale_kernel(n_total, keep_ref, recv_ref, *refs):
    sums, (out_hbm, out_ref, sems) = refs[:-3], refs[-3:]
    total = sums[0][...]
    for ref in sums[1:]:
        total += ref[...]
    core = lax.axis_index("col")
    rows = keep_ref.shape[0] // PIECES
    copies = []
    for i in range(PIECES):
        part = slice(i * rows, (i + 1) * rows)
        own = jnp.float32(n_total) * keep_ref[part, :] / total[0:1, :]
        other = jnp.float32(n_total) * recv_ref[part, :] / total[1:2, :]
        out_ref[part, :TILE] = jnp.where(core == 0, own, other)
        out_ref[part, TILE:] = jnp.where(core == 0, other, own)
        copies.append(
            pltpu.make_async_copy(out_ref.at[part, :], out_hbm.at[part, :], sems.at[i])
        )
        copies[-1].start()
    for copy in copies:
        copy.wait()


def scale(n_total, keep, recv, sums):
    shape = (keep.shape[0], 2 * TILE)
    return pl.pallas_call(
        functools.partial(scale_kernel, n_total),
        out_shape=struct(shape, jnp.float32),
        in_specs=[VMEM] * (2 + len(sums)),
        out_specs=pl.BlockSpec(memory_space=pl.ANY),
        scratch_shapes=[pltpu.VMEM(shape, jnp.float32), pltpu.SemaphoreType.DMA((PIECES,))],
        compiler_params=pltpu.CompilerParams(vmem_limit_bytes=8 * MIB),
    )(keep, recv, *sums)


def on_device(a_matrix, b_matrix, tile_map):
    n_total = a_matrix.shape[1] * 64
    half = ROWS // 2
    keep, send = call(split_kernel, [struct((half, TILE), b_matrix.dtype)] * 2, b_matrix)
    recv = swap(send)
    p = call(
        pack_kernel,
        struct((SLAB, TILE), a_matrix.dtype),
        tile_map.reshape(1, 16),
        a_matrix,
        first=SMEM,
    )
    a1, b1 = hop(p, 1, 0), hop(p, -1, 0)
    blocks = call(block_kernel, [struct((512, TILE), b_matrix.dtype)] * 4, after(keep, p), recv)
    far_y = hop(blocks[3], 0, 2)
    blocks = [blocks[0], hop(blocks[1], 0, 1), hop(blocks[2], 0, -1), far_y]
    wide = call(widen_kernel, struct((512, 4 * TILE), b_matrix.dtype), *blocks)

    a1, b1 = after(a1, wide), after(b1, wide)
    a3, a2, b2 = hop(a1, 2, 0), hop(a1, 1, 0), hop(b1, -1, 0)
    back, ahead = hop_x(wide, 1), hop_x(wide, -1)
    near = join([after(p, back, ahead), a1, b1, a2, b2, a3])
    near_other = swap(near)
    a4, b3 = hop(after(a3, back, ahead), 1, 0), hop(after(b2, back, ahead), -1, 0)
    across = hop_x(back, 1)

    panels = stack([wide, ahead, back], (0, 1, 3))
    near_steps, far_steps = (0, -1, 1, -2, 2, -3), (3, -4)
    held = (0, 1, 3)
    (total,) = product(panels, [near, near_other], [(0, held, near_steps), (1, held, near_steps)])
    far = join([after(b3, across, total), a4])
    far_other = swap(far)
    panels = stack([across], (2,), panels)
    every = (0, 1, 2, 3)
    rest = functools.partial(
        product,
        panels,
        [near, near_other, far, far_other],
        [(0, (2,), near_steps), (1, (2,), near_steps), (0, every, far_steps), (1, every, far_steps)],
        total,
    )

    low, high = rest(slots=(3,), outs=((0, 0, half), (0, half, half)))
    low, high = hop(low, 0, 1), hop(high, 0, 1)
    code, side = rest(slots=(1, 2), outs=((0, 0, ROWS), 1))
    sums = [hop(code, 0, -1)]
    sums.append(hop(relay(side, low, 0), 0, 1))
    sums.append(hop(relay(side, high, half), 0, 1))
    (own,) = rest(slots=(0,))
    keep, send, column = call(
        functools.partial(square_kernel, n_total / 32),
        [struct((half, TILE), jnp.float32)] * 2 + [struct((1, TILE), jnp.float32)],
        own,
        *sums,
    )
    column = jnp.concatenate([column, swap(column)])
    recv = swap(after(send, column))
    columns = [column] + [hop_x(column, d) for d in (1, -1, 2)]
    return scale(n_total, keep, recv, columns)


def solution(mesh):
    return jax.shard_map(
        on_device,
        mesh=mesh,
        in_specs=(
            P("row", ("col", "layer")),
            P(("col", "row"), "layer"),
            P("row", ("col", "layer")),
        ),
        out_specs=P(("row", "col"), "layer"),
        check_vma=False,
    )
```
